32 devices in a mesh: batch: 8 (over z, core), ctx: 4 (over y, x).
Axes of the slice: x: 2, y: 2, z: 4, core: 2. Of those that a mesh axis runs over, the one named last changes fastest.
Arguments:
- queries: bfloat16 [16384, 1024], P(('batch', 'ctx')), parts along dimension 0, may hold values from -6 to 6
- keys: bfloat16 [16384, 1024], P(('batch', 'ctx')), parts along dimension 0, may hold values from -6 to 6
- values: bfloat16 [16384, 2048], P(('batch', 'ctx')), parts along dimension 0, may hold values from -6 to 6
- out_grad: bfloat16 [16384, 2048], P(('batch', 'ctx')), parts along dimension 0, may hold values from -6 to 6
Outputs:
- attended: bfloat16 [16384, 2048], P(('batch', 'ctx')), parts along dimension 0
- query_grad: bfloat16 [16384, 1024], P(('batch', 'ctx')), parts along dimension 0
- key_grad: bfloat16 [16384, 1024], P(('batch', 'ctx')), parts along dimension 0
- value_grad: bfloat16 [16384, 2048], P(('batch', 'ctx')), parts along dimension 0
The draws below stay inside these ranges and needn't reach their ends.
There are 8 independent parts, one for each index of `batch`. The reference program is written for one: setup_inputs(seed, part) draws one part's arguments, and reference() takes and returns one part's arrays. A program takes and returns all parts, laid end to end along the dimension named above; each array names one. Nothing has to cross between parts.
All inputs are finite; a program needn't handle non-finite values.
Results may differ from the reference program's by a relative error of at most 0.0058.
Values sent between devices are 32-bit elements; how exact they have to be, the bound alone decides.
No kernel may reach another device: no remote copies, remote signals or barrier semaphores. Data moves between devices by JAX's collectives and lax.ppermute only.
A program may use at most 128 MiB of HBM per device.

```python
import jax
import jax.numpy as jnp
from jax import lax

H = 16
DK = 64
DV = 128
TOK_DEV = 512
SEQ = 2048
N_CTX = 4


def level_of(own_key, extent, cuts, least, largest):
    def one(axis_at, parts):
        draws = jax.random.uniform(jax.random.fold_in(jax.random.fold_in(own_key, 6), axis_at), (parts,), jnp.float32, least / len(cuts), largest / len(cuts))
        return jnp.repeat(jnp.exp(draws), extent[axis_at] // parts).reshape((-1,) + (1,) * (len(extent) - axis_at - 1))

    loudness = one(*cuts[0])
    for cut in cuts[1:]:
        loudness = loudness * one(*cut)
    return loudness


def noise(key, dims, scale, reach, cuts=(), dtype=jnp.bfloat16):
    entries = scale * jax.random.normal(key, dims, jnp.float32)
    if cuts:
        entries = entries * level_of(key, dims, cuts, -0.22, 0.18)
    return jnp.clip(entries, -reach, reach).astype(dtype)


def setup_inputs(seed: int = 0, part: int = 0) -> dict:
    splits = jax.random.split(jax.random.key(seed), 5)
    own_keys = jax.random.split(jax.random.fold_in(splits[4], part), 5)
    return {
        "queries": noise(own_keys[0], (SEQ, H * DK), 1.0, 6.0, ((0, 4),)),
        "keys": noise(own_keys[1], (SEQ, H * DK), 1.0, 6.0, ((0, 4),)),
        "values": noise(own_keys[2], (SEQ, H * DV), 1.0, 6.0, ((0, 4),)),
        "out_grad": noise(own_keys[3], (SEQ, H * DV), 1.0, 6.0, ((0, 4),)),
    }


def block_terms(inputs):
    query_h, key_h, value_h, scaled_grad, scales, prefix, suffix = inputs
    length = query_h.shape[0]
    causal = lax.iota(jnp.int32, length)[:, None] >= lax.iota(jnp.int32, length)[None, :]
    query_f = query_h.astype(jnp.float32)
    key_f = key_h.astype(jnp.float32)
    value_f = value_h.astype(jnp.float32)
    grad_f = scaled_grad.astype(jnp.float32)
    prefix_f = prefix.astype(jnp.float32)
    suffix_f = suffix.astype(jnp.float32)
    scores = jnp.einsum('thd,shd->hts', query_f, key_f)
    scores_bf = jnp.where(causal[None], scores, 0.0).astype(jnp.bfloat16).astype(jnp.float32)
    grad_scores = jnp.einsum('thc,shc->hts', grad_f, value_f)
    grad_bf = jnp.where(causal[None], grad_scores, 0.0).astype(jnp.bfloat16).astype(jnp.float32)
    attended = jnp.einsum('hts,shc->thc', scores_bf, value_f) + jnp.einsum('thd,hdc->thc', query_f, prefix_f)
    attended = (attended * scales[:, None, None]).astype(jnp.bfloat16)
    query_grad = jnp.einsum('hts,shd->thd', grad_bf, key_f) + jnp.einsum('thc,hdc->thd', grad_f, prefix_f)
    key_grad = jnp.einsum('hts,thd->shd', grad_bf, query_f) + jnp.einsum('shc,hdc->shd', value_f, suffix_f)
    value_grad = jnp.einsum('hts,thc->shc', scores_bf, grad_f) + jnp.einsum('shd,hdc->shc', key_f, suffix_f)
    return (attended, query_grad.astype(jnp.bfloat16), key_grad.astype(jnp.bfloat16), value_grad.astype(jnp.bfloat16))

def reference(queries, keys, values, out_grad):
    blocks = N_CTX
    length = TOK_DEV
    query_h = queries.reshape(blocks, length, H, DK)
    key_h = keys.reshape(blocks, length, H, DK)
    value_h = values.reshape(blocks, length, H, DV)
    grad_h = out_grad.reshape(blocks, length, H, DV)
    positions = lax.iota(jnp.int32, blocks * length).astype(jnp.float32).reshape(blocks, length)
    scales = 1.0 / jnp.sqrt(DK * (positions + 1.0))
    scaled_grad = (scales[:, :, None, None] * grad_h.astype(jnp.float32)).astype(jnp.bfloat16)
    key_value = jnp.einsum('bthd,bthc->bhdc', key_h.astype(jnp.float32), value_h.astype(jnp.float32))
    query_cot = jnp.einsum('bthd,bthc->bhdc', query_h.astype(jnp.float32), scaled_grad.astype(jnp.float32))
    empty = jnp.zeros((1, H, DK, DV), jnp.float32)
    prefix = jnp.concatenate([empty, jnp.cumsum(key_value, axis=0)[:-1]], axis=0).astype(jnp.bfloat16)
    reversed_sum = jnp.cumsum(query_cot[::-1], axis=0)[::-1]
    suffix = jnp.concatenate([reversed_sum[1:], empty], axis=0).astype(jnp.bfloat16)
    attended, query_grad, key_grad, value_grad = lax.map(block_terms, (query_h, key_h, value_h, scaled_grad, scales, prefix, suffix))
    total = blocks * length
    return (attended.reshape(total, H * DV), query_grad.reshape(total, H * DK), key_grad.reshape(total, H * DK), value_grad.reshape(total, H * DV))
```

```python
import functools

import jax
import jax.numpy as jnp
from jax import lax
from jax.experimental import pallas as pl
from jax.experimental.pallas import tpu as pltpu
from jax.sharding import PartitionSpec as P

H = 16
DK = 64
DV = 128
PAIRS = H // 2
HALF = PAIRS // 2
XW = 2 * DK
YW = 2 * DV
CHUNKS = 2
VMEM_LIMIT = 12 * 1024 * 1024

NT = (((1,), (1,)), ((), ()))
TN = (((0,), (0,)), ((), ()))
NN = (((1,), (0,)), ((), ()))


def dot(a, b, dims=NN):
    return lax.dot_general(a, b, dims, preferred_element_type=jnp.float32)


def is_low():
    size = lax.axis_size("ctx")
    if size != 4:
        return lax.axis_index("ctx") >= 0
    return lax.axis_index("ctx") < size // 2


def is_inner():
    at = lax.axis_index("ctx")
    return (at == 1) | (at == 2)


def row_scales(rows, first, columns):
    at = lax.axis_index("ctx") * rows[1] + first + lax.broadcasted_iota(jnp.int32, (rows[0], columns), 0)
    return 1.0 / jnp.sqrt(DK * (at.astype(jnp.float32) + 1.0))


def diagonal(square):
    return jnp.concatenate([square[:DK, :DV], square[DK:, DV:]], axis=0)


def states_kernel(first, forward, q, k, v, do, x, y, state, chunk_state, sems):
    low = is_low()
    plain = low if forward else jnp.logical_not(low)
    length = x.shape[1]

    def copies(a, b, p):
        return (
            pltpu.make_async_copy(a.at[:, pl.ds((first + p) * XW, XW)], x.at[p], sems.at[0, p]),
            pltpu.make_async_copy(b.at[:, pl.ds((first + p) * YW, YW)], y.at[p], sems.at[1, p]),
        )

    def run(a, b, scaled):
        for p in range(HALF):
            for c in copies(a, b, p):
                c.start()
        if scaled:
            scales = row_scales((length, length), 0, YW)
        for p in range(HALF):
            for c in copies(a, b, p):
                c.wait()
            if scaled:
                y[p] = (y[p].astype(jnp.float32) * scales).astype(jnp.bfloat16)
            size = length // CHUNKS
            parts = [
                diagonal(dot(x[p, c * size : (c + 1) * size, :], y[p, c * size : (c + 1) * size, :], TN))
                for c in range(CHUNKS)
            ]
            state[p] = parts[0] + parts[1]
            chunk_state[p] = parts[1] if scaled else parts[0]

    @pl.when(plain)
    def _():
        run(k, v, False)

    @pl.when(jnp.logical_not(plain))
    def _():
        run(q, do, True)


def states(first, forward, q, k, v, do):
    length = q.shape[0]
    any_spec = pl.BlockSpec(memory_space=pltpu.HBM)
    vmem = pl.BlockSpec(memory_space=pltpu.VMEM)
    return pl.pallas_call(
        functools.partial(states_kernel, first, forward),
        in_specs=[any_spec] * 4,
        out_specs=[vmem, vmem, vmem, vmem],
        out_shape=[
            pltpu.VMEM((HALF, length, XW), jnp.bfloat16),
            pltpu.VMEM((HALF, length, YW), jnp.bfloat16),
            jax.ShapeDtypeStruct((HALF, XW, DV), jnp.float32),
            pltpu.VMEM((HALF, XW, DV), jnp.float32),
        ],
        scratch_shapes=[pltpu.SemaphoreType.DMA((2, HALF))],
        compiler_params=pltpu.CompilerParams(vmem_limit_bytes=VMEM_LIMIT),
        cost_estimate=pl.CostEstimate(flops=2 * HALF * length * XW * YW, bytes_accessed=HALF * length * (XW + YW) * 4, transcendentals=0),
        name="states",
    )(q, k, v, do)


def head_lanes(array):
    lane = lax.broadcasted_iota(jnp.int32, array.shape, 1)
    zero = jnp.zeros_like(array)
    return jnp.where(lane < DK, array, zero), jnp.where(lane >= DK, array, zero)


def block_diagonal(state):
    row = lax.broadcasted_iota(jnp.int32, state.shape, 0)
    zero = jnp.zeros_like(state)
    both = jnp.concatenate([jnp.where(row < DK, state, zero), jnp.where(row >= DK, state, zero)], axis=1)
    return both.astype(jnp.bfloat16)


def send_out(staged, first, p, width, sem, when_low, when_high, low):
    columns = pl.ds(pl.multiple_of((first + p) * width, width), width)
    to_low = pltpu.make_async_copy(staged.at[p], when_low.at[:, columns], sem.at[p])
    to_high = pltpu.make_async_copy(staged.at[p], when_high.at[:, columns], sem.at[p])

    @pl.when(low)
    def _():
        to_low.start()

    @pl.when(jnp.logical_not(low))
    def _():
        to_high.start()


def wait_out(staged, first, p, width, sem, when_low):
    columns = pl.ds(pl.multiple_of((first + p) * width, width), width)
    pltpu.make_async_copy(staged.at[p], when_low.at[:, columns], sem.at[p]).wait()


def local_kernel(first, *refs):
    xf, yf, xg, yg, fsel, near = refs[:6]
    att, qg, kg, vg, o2, o4, o1_out, o3_out, sem1, sem3 = refs[-10:]
    low = is_low()
    length = xf.shape[1]
    size = length // CHUNKS
    row = lax.broadcasted_iota(jnp.int32, (size, size), 0)
    col = lax.broadcasted_iota(jnp.int32, (size, size), 1)
    keep = jnp.where(low, row - col, col - row) >= 0
    has_near = is_inner()

    def body(p, carry):
        base = near[p]
        if lax.axis_size("ctx") == 4:
            base = jnp.where(has_near, base, 0.0)
        added = fsel[p]
        for c in range(CHUNKS):
            rows = pl.ds(c * size, size)
            takes = low if c == 1 else jnp.logical_not(low)
            bd = block_diagonal(base + jnp.where(takes, added, 0.0))
            xf_c, xg_c, yf_c, yg_c = xf[p, rows, :], xg[p, rows, :], yf[p, rows, :], yg[p, rows, :]
            xf_h, xg_h = head_lanes(xf_c), head_lanes(xg_c)
            o1 = dot(xg_c, bd)
            o3 = dot(yg_c, bd, NT)
            o4_c = None
            for h in range(2):
                lanes = slice(h * DV, (h + 1) * DV)
                m = jnp.where(keep, dot(xg_c, xf_h[h], NT), 0.0).astype(jnp.bfloat16)
                n = jnp.where(keep, dot(yg_c[:, lanes], yf_c[:, lanes], NT), 0.0).astype(jnp.bfloat16)
                o1_h = o1[:, lanes] + dot(m, yf_c[:, lanes])
                scale = jnp.where(low, row_scales((size, length), c * size, DV), 1.0)
                o1_out[p, rows, lanes] = (o1_h * scale).astype(jnp.bfloat16)
                o2[p, rows, lanes] = dot(m, yg_c[:, lanes], TN)
                o3 += dot(n, xf_h[h])
                part = dot(n, xg_h[h], TN)
                o4_c = part if o4_c is None else o4_c + part
            o3_out[p, rows, :] = o3.astype(jnp.bfloat16)
            o4[p, rows, :] = o4_c
        send_out(o1_out, first, p, YW, sem1, att, vg, low)
        send_out(o3_out, first, p, XW, sem3, qg, kg, low)
        return carry

    lax.fori_loop(0, HALF, body, 0)
    for p in range(HALF):
        wait_out(o1_out, first, p, YW, sem1, att)
        wait_out(o3_out, first, p, XW, sem3, qg)


def far_kernel(first, *refs):
    xf, yf, gsel, far1, far2, o2, o4 = refs[:7]
    att, qg, kg, vg, o2_out, o4_out, sem2, sem4 = refs[-8:]
    low = is_low()
    length = xf.shape[1]
    size = length // CHUNKS
    special = lax.axis_size("ctx") == 4
    first_half = first == 0

    def body(p, carry):
        base = far1[p]
        if special:
            if first_half:
                base += jnp.where(is_inner(), 0.0, far2[p])
            else:
                base += far2[p]
        added = gsel[p]
        for c in range(CHUNKS):
            rows = pl.ds(c * size, size)
            takes = low if c == 0 else jnp.logical_not(low)
            bd = block_diagonal(base + jnp.where(takes, added, 0.0))
            out2 = o2[p, rows, :] + dot(xf[p, rows, :], bd)
            scale = jnp.where(low, 1.0, row_scales((size, length), c * size, YW))
            o2_out[p, rows, :] = (out2 * scale).astype(jnp.bfloat16)
            out4 = o4[p, rows, :] + dot(yf[p, rows, :], bd, NT)
            o4_out[p, rows, :] = out4.astype(jnp.bfloat16)
        send_out(o2_out, first, p, YW, sem2, vg, att, low)
        send_out(o4_out, first, p, XW, sem4, kg, qg, low)
        return carry

    lax.fori_loop(0, HALF, body, 0)
    for p in range(HALF):
        wait_out(o2_out, first, p, YW, sem2, vg)
        wait_out(o4_out, first, p, XW, sem4, kg)


def in_vmem(array):
    return pltpu.with_memory_space_constraint(array, pltpu.VMEM)


ANY = pl.BlockSpec(memory_space=pltpu.HBM)
WHOLE = pl.BlockSpec(memory_space=pltpu.VMEM)


def out_shapes(length):
    wide = jax.ShapeDtypeStruct((length, H * DV), jnp.bfloat16)
    narrow = jax.ShapeDtypeStruct((length, H * DK), jnp.bfloat16)
    return [wide, narrow, narrow, wide]


def local_terms(first, f, g, near, outs):
    xf, yf, _, fsel = f
    xg, yg, _, _ = g
    length = xf.shape[1]
    scratch = [
        pltpu.VMEM((HALF, length, YW), jnp.bfloat16),
        pltpu.VMEM((HALF, length, XW), jnp.bfloat16),
        pltpu.SemaphoreType.DMA((HALF,)),
        pltpu.SemaphoreType.DMA((HALF,)),
    ]
    ins = [in_vmem(xf), in_vmem(yf), in_vmem(xg), in_vmem(yg), in_vmem(fsel), near]
    return pl.pallas_call(
        functools.partial(local_kernel, first),
        in_specs=[WHOLE] * 6 + [ANY] * len(outs),
        out_specs=[ANY] * 4 + [WHOLE] * 2,
        out_shape=out_shapes(length)
        + [pltpu.VMEM((HALF, length, YW), jnp.float32), pltpu.VMEM((HALF, length, XW), jnp.float32)],
        input_output_aliases={6 + i: i for i in range(len(outs))},
        scratch_shapes=scratch,
        compiler_params=pltpu.CompilerParams(vmem_limit_bytes=VMEM_LIMIT),
        cost_estimate=pl.CostEstimate(flops=HALF * 2 * 12 * 2 * 256**3 // 2, bytes_accessed=4 * 1024 * 1024, transcendentals=0),
        name="local",
    )(*ins, *outs)


def far_terms(first, f, g, far1, far2, o2, o4, outs):
    xf, yf, _, _ = f
    gsel = g[3]
    length = xf.shape[1]
    scratch = [
        pltpu.VMEM((HALF, length, YW), jnp.bfloat16),
        pltpu.VMEM((HALF, length, XW), jnp.bfloat16),
        pltpu.SemaphoreType.DMA((HALF,)),
        pltpu.SemaphoreType.DMA((HALF,)),
    ]
    ins = [in_vmem(xf), in_vmem(yf), in_vmem(gsel), far1, far2, in_vmem(o2), in_vmem(o4)]
    return pl.pallas_call(
        functools.partial(far_kernel, first),
        in_specs=[WHOLE] * 7 + [ANY] * 4,
        out_specs=[ANY] * 4,
        out_shape=out_shapes(length),
        input_output_aliases={7 + i: i for i in range(4)},
        scratch_shapes=scratch,
        compiler_params=pltpu.CompilerParams(vmem_limit_bytes=VMEM_LIMIT),
        cost_estimate=pl.CostEstimate(flops=HALF * 4 * 2 * 256**3 // 2, bytes_accessed=2 * 1024 * 1024, transcendentals=0),
        name="far",
    )(*ins, *outs)


def scan_sum(state, size, reverse):
    step, total = 1, state
    sign = -1 if reverse else 1
    before = lax.ppermute(state, "ctx", [(i, i + sign) for i in range(size) if 0 <= i + sign < size])
    total = before
    while step < size:
        moved = [(i, i + sign * step) for i in range(size) if 0 <= i + sign * step < size]
        total = total + lax.ppermute(total, "ctx", moved)
        step *= 2
    return total


def local(queries, keys, values, out_grad):
    args = [pltpu.with_memory_space_constraint(a, pltpu.HBM) for a in (queries, keys, values, out_grad)]
    size = lax.axis_size("ctx")
    fa = states(0, True, *args)
    fb = states(HALF, True, *args)
    ga = states(0, False, *args)
    gb = states(HALF, False, *args)
    if size == 4:
        swap_x = [(0, 1), (1, 0), (2, 3), (3, 2)]
        swap_y = [(0, 2), (2, 0), (1, 3), (3, 1)]
        inner = is_inner()
        got_xa = lax.ppermute(fa[2], "ctx", swap_x)
        got_y1 = lax.ppermute(fb[2], "ctx", swap_y)
        got_xb = lax.ppermute(jnp.where(inner, ga[2], fb[2]), "ctx", swap_x)
        got_y2 = lax.ppermute(fa[2] + got_xa, "ctx", swap_y)
        got_x2 = lax.ppermute(got_y1 + jnp.where(inner, gb[2], 0.0), "ctx", swap_x)
        near_a, near_b = got_xa, got_xb
        far_a, far_b = (got_y2, got_xb), (got_y1, got_x2)
    else:
        near_a, near_b = scan_sum(fa[2], size, False), scan_sum(fb[2], size, False)
        far_a, far_b = [scan_sum(ga[2], size, True)] * 2, [scan_sum(gb[2], size, True)] * 2
    *outs, o2a, o4a = local_terms(0, fa, ga, near_a, [])
    *outs, o2b, o4b = local_terms(HALF, fb, gb, near_b, outs)
    outs = far_terms(0, fa, ga, *far_a, o2a, o4a, outs)
    outs = far_terms(HALF, fb, gb, *far_b, o2b, o4b, outs)
    return tuple(outs)


def solution(mesh):
    spec = P(("batch", "ctx"), None)
    return jax.shard_map(local, mesh=mesh, in_specs=(spec,) * 4, out_specs=(spec,) * 4, check_vma=False)
```

```python
import functools

import jax
import jax.numpy as jnp
from jax import lax
from jax.experimental import pallas as pl
from jax.experimental.pallas import tpu as pltpu
from jax.sharding import PartitionSpec as P


H = 16
DK = 64
DV = 128
PAIRS = H // 2
HALF = PAIRS // 2
XW = 2 * DK
YW = 2 * DV
CHUNK = 128
SPLIT = 2
VMEM_LIMIT = 12 * 1024 * 1024

NN = (((1,), (0,)), ((), ()))
NT = (((1,), (1,)), ((), ()))
TN = (((0,), (0,)), ((), ()))
F32 = jnp.float32
BF16 = jnp.bfloat16

HBM = pl.BlockSpec(memory_space=pltpu.HBM)
VMEM = pl.BlockSpec(memory_space=pltpu.VMEM)


def dot(a, b, dims=NN):
    return lax.dot_general(a, b, dims, preferred_element_type=F32)


def is_low():
    size = lax.axis_size("ctx")
    return lax.axis_index("ctx") < (size // 2 if size == 4 else size)


def is_inner():
    at = lax.axis_index("ctx")
    return (at == 1) | (at == 2) if lax.axis_size("ctx") == 4 else at >= 0


def in_vmem(array):
    return pltpu.with_memory_space_constraint(array, pltpu.VMEM)


def in_hbm(array):
    return pltpu.with_memory_space_constraint(array, pltpu.HBM)


def x_shape(length, dtype=BF16):
    return pltpu.VMEM((HALF, length, XW), dtype)


def y_shape(length, dtype=BF16):
    return pltpu.VMEM((HALF, length, YW), dtype)


STATE = pltpu.VMEM((HALF, XW, DV), F32)


def steps_shape(length):
    return pltpu.VMEM((HALF, length // CHUNK, XW, DV), F32)


def params():
    return pltpu.CompilerParams(vmem_limit_bytes=VMEM_LIMIT)


def diagonal(square):
    return jnp.concatenate([square[:DK, :DV], square[DK:, DV:]], axis=0)


def pair_states(x, y, scaled, scale, backward, steps):
    count = y.shape[0] // CHUNK
    parts = []
    for c in range(count):
        rows = slice(c * CHUNK, (c + 1) * CHUNK)
        s = scale[rows, :]
        new = (y[rows, :].astype(F32) * jnp.concatenate([s, s], axis=1)).astype(BF16)
        scaled[rows, :] = new
        parts.append(diagonal(dot(x[rows, :], new, TN)))
    before, after = [jnp.zeros_like(parts[0])], [jnp.zeros_like(parts[0])]
    for c in range(count - 1):
        before.append(before[-1] + parts[c])
        after.append(after[-1] + parts[count - 1 - c])
    for c in range(count):
        steps[c] = jnp.where(backward, after[count - 1 - c], before[c])
    return before[-1] + parts[-1]


def load_kernel(q, k, v, do, xfa, yfa, xfb, yfb, xga, yga, xgb, ygb, scale_low, scale_high, state, steps, raw, sems):
    low = is_low()
    length = q.shape[0]

    def copies(a, b, x, y, first, at):
        return [
            copy
            for p in range(HALF)
            for copy in (
                pltpu.make_async_copy(a.at[:, pl.ds((first + p) * XW, XW)], x.at[p], sems.at[at, 0, p]),
                pltpu.make_async_copy(b.at[:, pl.ds((first + p) * YW, YW)], y.at[p], sems.at[at, 1, p]),
            )
        ]

    def start(f, g):
        for a, b, x, y, first, at in (
            (*f, xfa, raw, 0, 0),
            (*f, xfb, yfb, HALF, 1),
            (*g, xga, yga, 0, 2),
            (*g, xgb, ygb, HALF, 3),
        ):
            for copy in copies(a, b, x, y, first, at):
                copy.start()

    @pl.when(low)
    def _():
        start((k, v), (q, do))

    @pl.when(jnp.logical_not(low))
    def _():
        start((q, do), (k, v))

    at = lax.axis_index("ctx") * length + lax.broadcasted_iota(jnp.int32, (length, DV), 0)
    scale = 1.0 / jnp.sqrt(DK * (at.astype(F32) + 1.0))
    scale_low[...] = jnp.where(low, scale, 1.0)
    scale_high[...] = jnp.where(low, 1.0, scale)
    first = copies(k, v, xfa, raw, 0, 0)
    for p in range(HALF):
        first[2 * p].wait()
        first[2 * p + 1].wait()
        state[p] = pair_states(xfa.at[p], raw.at[p], yfa.at[p], scale_high, jnp.logical_not(low), steps.at[p])
    for x, y, at in ((xfb, yfb, 1), (xga, yga, 2), (xgb, ygb, 3)):
        for copy in copies(k, v, x, y, 0, at):
            copy.wait()


def load(q, k, v, do):
    length = q.shape[0]
    x, y = x_shape(length), y_shape(length)
    scale = pltpu.VMEM((length, DV), F32)
    return pl.pallas_call(
        load_kernel,
        in_specs=[HBM] * 4,
        out_specs=[VMEM] * 12,
        out_shape=[x, y, x, y, x, y, x, y, scale, scale, STATE, steps_shape(length)],
        scratch_shapes=[y, pltpu.SemaphoreType.DMA((4, 2, HALF))],
        compiler_params=params(),
        name="load",
    )(q, k, v, do)


def f_kernel(x, y, scale, scaled, state, steps):
    high = jnp.logical_not(is_low())
    for p in range(HALF):
        state[p] = pair_states(x.at[p], y.at[p], scaled.at[p], scale, high, steps.at[p])


def f_states(x, y, scale):
    length = x.shape[1]
    return pl.pallas_call(
        f_kernel,
        in_specs=[VMEM] * 3,
        out_specs=[VMEM] * 3,
        out_shape=[y_shape(length), STATE, steps_shape(length)],
        compiler_params=params(),
        name="f_states",
    )(in_vmem(x), in_vmem(y), in_vmem(scale))


def g_kernel(xa, ya, xb, yb, scale, fb, scaled_a, scaled_b, steps_a, steps_b, mixed, inner_b):
    low = is_low()
    inner = is_inner()
    for p in range(HALF):
        state = pair_states(xa.at[p], ya.at[p], scaled_a.at[p], scale, low, steps_a.at[p])
        mixed[p] = jnp.where(inner, state, fb[p])
    for p in range(HALF):
        state = pair_states(xb.at[p], yb.at[p], scaled_b.at[p], scale, low, steps_b.at[p])
        inner_b[p] = jnp.where(inner, state, 0.0)


def g_states(xa, ya, xb, yb, scale, fb):
    length = xa.shape[1]
    y, steps = y_shape(length), steps_shape(length)
    return pl.pallas_call(
        g_kernel,
        in_specs=[VMEM] * 6,
        out_specs=[VMEM] * 6,
        out_shape=[y, y, steps, steps, STATE, STATE],
        compiler_params=params(),
        name="g_states",
    )(*map(in_vmem, (xa, ya, xb, yb, scale, fb)))


def add(a, b, parts, after=()):
    shape = pltpu.VMEM((HALF // parts, XW, DV), F32)
    return pl.pallas_call(
        functools.partial(add_parts_kernel, parts),
        in_specs=[VMEM] * 2 + [HBM] * len(after),
        out_specs=[VMEM] * parts,
        out_shape=[shape] * parts,
        compiler_params=params(),
        name="add",
    )(a, b, *after)


def add_parts_kernel(parts, a, b, *refs):
    outs = refs[-parts:]
    count = a.shape[0] // parts
    for i, out in enumerate(outs):
        for p in range(count):
            out[p] = a[i * count + p] + b[i * count + p]


def head_rows(x):
    lane = lax.broadcasted_iota(jnp.int32, x.shape, 1)
    zero = jnp.zeros_like(x)
    return jnp.concatenate([jnp.where(lane < DK, x, zero), jnp.where(lane >= DK, x, zero)], axis=0)


def head_blocks(y):
    zero = jnp.zeros_like(y[:, :DV])
    top = jnp.concatenate([y[:, :DV], zero], axis=1)
    return jnp.concatenate([top, jnp.concatenate([zero, y[:, DV:]], axis=1)], axis=0)


def state_blocks(state):
    row = lax.broadcasted_iota(jnp.int32, state.shape, 0)
    zero = jnp.zeros_like(state)
    both = jnp.concatenate([jnp.where(row < DK, state, zero), jnp.where(row >= DK, state, zero)], axis=1)
    return both.astype(BF16)


def turned(scores):
    return jnp.concatenate([scores[:, :CHUNK].T, scores[:, CHUNK:].T], axis=1)


def send(staged, p, when_low, when_high, columns, sem, low):
    to_low = pltpu.make_async_copy(staged.at[p], when_low.at[:, columns], sem.at[p])
    to_high = pltpu.make_async_copy(staged.at[p], when_high.at[:, columns], sem.at[p])

    @pl.when(low)
    def _():
        to_low.start()

    @pl.when(jnp.logical_not(low))
    def _():
        to_high.start()


def local_kernel(first, xf, yf, xg, yg, steps, near, scale, *refs):
    att, qg, kg, vg, o2, o4, o1_out, o3_out, sem1, sem3 = refs[-10:]
    low = is_low()
    inner = is_inner()
    row = lax.broadcasted_iota(jnp.int32, (CHUNK, 2 * CHUNK), 0)
    col = lax.rem(lax.broadcasted_iota(jnp.int32, (CHUNK, 2 * CHUNK), 1), CHUNK)
    keep = jnp.where(low, row - col, col - row) >= 0
    chunks = [slice(c, c + CHUNK) for c in range(0, xf.shape[1], CHUNK)]
    for p in range(HALF):
        base = jnp.where(inner, near[p], 0.0)
        parts, scores = [], []
        for c, rows in enumerate(chunks):
            x1, y1, x2, y2 = xf[p, rows, :], yf[p, rows, :], xg[p, rows, :], yg[p, rows, :]
            s = scale[rows, :]
            blocks = state_blocks(base + steps[p, c])
            parts.append((head_rows(x1), head_blocks(y1), x2, y2, jnp.concatenate([s, s], axis=1), blocks))
        for x1s, y1s, x2, y2, _, _ in parts:
            m = jnp.where(keep, dot(x2, x1s, NT), 0.0).astype(BF16)
            n = jnp.where(keep, dot(y2, y1s, NT), 0.0).astype(BF16)
            scores.append((m, n))
        for rows, (x1s, y1s, x2, y2, s, blocks), (m, n) in zip(chunks, parts, scores):
            o1_out[p, rows, :] = ((dot(m, y1s) + dot(x2, blocks)) * s).astype(BF16)
            o3_out[p, rows, :] = (dot(n, x1s) + dot(y2, blocks, NT)).astype(BF16)
            o2[p, rows, :] = dot(turned(m), head_blocks(y2))
            o4[p, rows, :] = dot(turned(n), head_rows(x2))
        send(o1_out, p, att, vg, pl.ds((first + p) * YW, YW), sem1, low)
        send(o3_out, p, qg, kg, pl.ds((first + p) * XW, XW), sem3, low)
    for p in range(HALF):
        pltpu.make_async_copy(o1_out.at[p], att.at[:, pl.ds((first + p) * YW, YW)], sem1.at[p]).wait()
        pltpu.make_async_copy(o3_out.at[p], qg.at[:, pl.ds((first + p) * XW, XW)], sem3.at[p]).wait()


def out_shapes(length):
    wide = jax.ShapeDtypeStruct((length, H * DV), BF16)
    narrow = jax.ShapeDtypeStruct((length, H * DK), BF16)
    return [wide, narrow, narrow, wide]


def local_terms(first, xf, yf, xg, yg, steps, near, scale, outs, after):
    length = xf.shape[1]
    ins = [*map(in_vmem, (xf, yf, xg, yg, steps)), near, in_vmem(scale)]
    return pl.pallas_call(
        functools.partial(local_kernel, first),
        in_specs=[VMEM] * 7 + [HBM] * (len(outs) + len(after)),
        out_specs=[HBM] * 4 + [VMEM] * 2,
        out_shape=out_shapes(length) + [y_shape(length, F32), x_shape(length, F32)],
        input_output_aliases={7 + i: i for i in range(len(outs))},
        scratch_shapes=[
            y_shape(length),
            x_shape(length),
            pltpu.SemaphoreType.DMA((HALF,)),
            pltpu.SemaphoreType.DMA((HALF,)),
        ],
        compiler_params=params(),
        name="local",
    )(*ins, *outs, *after)


def far_kernel(first, offset, count, mask_second, xf, yf, steps, far1, far2, o2, o4, scale, *refs):
    att, qg, kg, vg, o2_out, o4_out, sem2, sem4 = refs[-8:]
    low = is_low()
    inner = is_inner()
    chunks = [slice(c, c + CHUNK) for c in range(0, xf.shape[1], CHUNK)]
    for i in range(count):
        p = offset + i
        second = far2[i]
        base = far1[p] + (jnp.where(inner, 0.0, second) if mask_second else second)
        blocks = [state_blocks(base + steps[p, c]) for c in range(len(chunks))]
        wide = [dot(xf[p, rows, :], b) for rows, b in zip(chunks, blocks)]
        narrow = [dot(yf[p, rows, :], b, NT) for rows, b in zip(chunks, blocks)]
        for rows, a in zip(chunks, wide):
            s = scale[rows, :]
            o2_out[i, rows, :] = ((o2[p, rows, :] + a) * jnp.concatenate([s, s], axis=1)).astype(BF16)
        send(o2_out, i, vg, att, pl.ds((first + p) * YW, YW), sem2, low)
        for rows, a in zip(chunks, narrow):
            o4_out[i, rows, :] = (o4[p, rows, :] + a).astype(BF16)
        send(o4_out, i, kg, qg, pl.ds((first + p) * XW, XW), sem4, low)
    for i in range(count):
        p = offset + i
        pltpu.make_async_copy(o2_out.at[i], vg.at[:, pl.ds((first + p) * YW, YW)], sem2.at[i]).wait()
        pltpu.make_async_copy(o4_out.at[i], kg.at[:, pl.ds((first + p) * XW, XW)], sem4.at[i]).wait()


def far_terms(first, offset, count, mask_second, xf, yf, steps, far1, far2, o2, o4, scale, outs):
    length = xf.shape[1]
    ins = [*map(in_vmem, (xf, yf, steps)), far1, far2, *map(in_vmem, (o2, o4, scale))]
    return pl.pallas_call(
        functools.partial(far_kernel, first, offset, count, mask_second),
        in_specs=[VMEM] * 8 + [HBM] * 4,
        out_specs=[HBM] * 4,
        out_shape=out_shapes(length),
        input_output_aliases={8 + i: i for i in range(4)},
        scratch_shapes=[
            pltpu.VMEM((count, length, YW), BF16),
            pltpu.VMEM((count, length, XW), BF16),
            pltpu.SemaphoreType.DMA((count,)),
            pltpu.SemaphoreType.DMA((count,)),
        ],
        compiler_params=params(),
        name="far",
    )(*ins, *outs)


def scan_sum(state, size, sign):
    def moved(array, step):
        return lax.ppermute(array, "ctx", [(i, i + sign * step) for i in range(size) if 0 <= i + sign * step < size])

    total, step = moved(state, 1), 1
    while step < size:
        total, step = total + moved(total, step), 2 * step
    return total


def local(queries, keys, values, out_grad):
    size = lax.axis_size("ctx")
    xfa, yfa, xfb, yfb, xga, yga, xgb, ygb, scale_low, scale_high, fa, fa_steps = load(
        *map(in_hbm, (queries, keys, values, out_grad))
    )
    swap_x = [(0, 1), (1, 0), (2, 3), (3, 2)]
    swap_y = [(0, 2), (2, 0), (1, 3), (3, 1)]
    if size == 4:
        got_xa = lax.ppermute(fa, "ctx", swap_x)
    yfb, fb, fb_steps = f_states(xfb, yfb, scale_high)
    if size == 4:
        got_y1 = lax.ppermute(fb, "ctx", swap_y)
    yga, ygb, ga_steps, gb_steps, mixed, inner_b = g_states(xga, yga, xgb, ygb, scale_low, fb)
    if size == 4:
        got_xb = lax.ppermute(mixed, "ctx", swap_x)
        (sum_a,) = add(fa, got_xa, 1)
        got_y2 = lax.ppermute(sum_a, "ctx", swap_y)
        near_a, near_b, first_token = got_xa, got_xb, [sum_a]
        far_a, far_b = (got_y2, got_xb), got_y1
    else:
        near_a, near_b, first_token = scan_sum(fa, size, 1), scan_sum(fb, size, 1), []
        far_a, far_b = (scan_sum(mixed, size, -1), mixed), scan_sum(inner_b, size, -1)
    *outs, o2a, o4a = local_terms(0, xfa, yfa, xga, yga, fa_steps, near_a, scale_low, [], first_token)
    if size == 4:
        sums = add(got_y1, inner_b, SPLIT, [outs[1]])
        far_last = [lax.ppermute(s, "ctx", swap_x) for s in sums]
        second_token = list(sums)
    else:
        far_last, second_token = [jnp.zeros((HALF // SPLIT, XW, DV), F32)] * SPLIT, []
    *outs, o2b, o4b = local_terms(HALF, xfb, yfb, xgb, ygb, fb_steps, near_b, scale_low, outs, second_token)
    outs = far_terms(0, 0, HALF, True, xfa, yfa, ga_steps, *far_a, o2a, o4a, scale_high, outs)
    count = HALF // SPLIT
    for i in range(SPLIT):
        outs = far_terms(
            HALF, i * count, count, False, xfb, yfb, gb_steps, far_b, far_last[i], o2b, o4b, scale_high, outs
        )
    return tuple(outs)


def solution(mesh):
    spec = P(("batch", "ctx"), None)
    return jax.shard_map(local, mesh=mesh, in_specs=(spec,) * 4, out_specs=(spec,) * 4, check_vma=False)
```

```python
import functools

import jax
import jax.numpy as jnp
from jax import lax
from jax.experimental import pallas as pl
from jax.experimental.pallas import tpu as pltpu
from jax.sharding import PartitionSpec as P


H = 16
DK = 64
DV = 128
PAIRS = H // 2
HALF = PAIRS // 2
XW = 2 * DK
YW = 2 * DV
CHUNK = 128
SPLIT = 2
VMEM_LIMIT = 12 * 1024 * 1024

NN = (((1,), (0,)), ((), ()))
NT = (((1,), (1,)), ((), ()))
TN = (((0,), (0,)), ((), ()))
F32 = jnp.float32
BF16 = jnp.bfloat16

HBM = pl.BlockSpec(memory_space=pltpu.HBM)
VMEM = pl.BlockSpec(memory_space=pltpu.VMEM)


def dot(a, b, dims=NN):
    return lax.dot_general(a, b, dims, preferred_element_type=F32)


def is_low():
    size = lax.axis_size("ctx")
    return lax.axis_index("ctx") < (size // 2 if size == 4 else size)


def is_inner():
    at = lax.axis_index("ctx")
    return (at == 1) | (at == 2) if lax.axis_size("ctx") == 4 else at >= 0


def in_vmem(array):
    return pltpu.with_memory_space_constraint(array, pltpu.VMEM)


def in_hbm(array):
    return pltpu.with_memory_space_constraint(array, pltpu.HBM)


def x_shape(length, dtype=BF16):
    return pltpu.VMEM((length, HALF * XW), dtype)


def y_shape(length, dtype=BF16):
    return pltpu.VMEM((length, HALF * YW), dtype)


STATE = pltpu.VMEM((HALF, XW, DV), F32)


def steps_shape(length):
    return pltpu.VMEM((HALF, length // CHUNK, XW, DV), F32)


def params():
    return pltpu.CompilerParams(vmem_limit_bytes=VMEM_LIMIT)


def diagonal(square):
    return jnp.concatenate([square[:DK, :DV], square[DK:, DV:]], axis=0)


def xs(p):
    return slice(p * XW, (p + 1) * XW)


def ys(p):
    return slice(p * YW, (p + 1) * YW)


def chunks_of(array):
    return [slice(c, c + CHUNK) for c in range(0, array.shape[0], CHUNK)]


def twice(scale):
    return jnp.concatenate([scale, scale], axis=1)


def chunk_states(x, y, scaled, scale, rows):
    s = twice(scale[rows, :])
    states = []
    for p in range(HALF):
        new = (y[rows, ys(p)].astype(F32) * s).astype(BF16)
        scaled[rows, ys(p)] = new
        states.append(diagonal(dot(x[rows, xs(p)], new, TN)))
    return states


def block_states(parts, backward, steps):
    count = len(parts)
    states = []
    for p in range(HALF):
        zero = jnp.zeros_like(parts[0][p])
        before, after = [zero], [zero]
        for c in range(count - 1):
            before.append(before[-1] + parts[c][p])
            after.append(after[-1] + parts[count - 1 - c][p])
        for c in range(count):
            steps[p, c] = jnp.where(backward, after[count - 1 - c], before[c])
        states.append(before[-1] + parts[-1][p])
    return states


def load_kernel(q, k, v, do, xfa, yfa, xfb, yfb, xga, yga, xgb, ygb, scale_low, scale_high, state, steps, raw, sems):
    low = is_low()
    length = q.shape[0]
    chunks = chunks_of(q)

    def copies(a, b, x, y, half, at):
        wide, narrow = pl.ds(half * HALF * YW, HALF * YW), pl.ds(half * HALF * XW, HALF * XW)
        return [
            (
                pltpu.make_async_copy(a.at[rows, narrow], x.at[rows, :], sems.at[at, 0, c]),
                pltpu.make_async_copy(b.at[rows, wide], y.at[rows, :], sems.at[at, 1, c]),
            )
            for c, rows in enumerate(chunks)
        ]

    def start(f, g):
        for a, b, x, y, half, at in (
            (*f, xfa, raw, 0, 0),
            (*f, xfb, yfb, 1, 1),
            (*g, xga, yga, 0, 2),
            (*g, xgb, ygb, 1, 3),
        ):
            for pair in copies(a, b, x, y, half, at):
                for copy in pair:
                    copy.start()

    @pl.when(low)
    def _():
        start((k, v), (q, do))

    @pl.when(jnp.logical_not(low))
    def _():
        start((q, do), (k, v))

    at = lax.axis_index("ctx") * length + lax.broadcasted_iota(jnp.int32, (length, DV), 0)
    scale = 1.0 / jnp.sqrt(DK * (at.astype(F32) + 1.0))
    scale_low[...] = jnp.where(low, scale, 1.0)
    scale_high[...] = jnp.where(low, 1.0, scale)
    parts = []
    for rows, pair in zip(chunks, copies(k, v, xfa, raw, 0, 0)):
        for copy in pair:
            copy.wait()
        parts.append(chunk_states(xfa, raw, yfa, scale_high, rows))
    for p, new in enumerate(block_states(parts, jnp.logical_not(low), steps)):
        state[p] = new
    for x, y, at in ((xfb, yfb, 1), (xga, yga, 2), (xgb, ygb, 3)):
        for pair in copies(k, v, x, y, 0, at):
            for copy in pair:
                copy.wait()


def load(q, k, v, do):
    length = q.shape[0]
    x, y = x_shape(length), y_shape(length)
    scale = pltpu.VMEM((length, DV), F32)
    return pl.pallas_call(
        load_kernel,
        in_specs=[HBM] * 4,
        out_specs=[VMEM] * 12,
        out_shape=[x, y, x, y, x, y, x, y, scale, scale, STATE, steps_shape(length)],
        scratch_shapes=[y, pltpu.SemaphoreType.DMA((4, 2, length // CHUNK))],
        compiler_params=params(),
        name="load",
    )(q, k, v, do)


def f_kernel(x, y, scale, scaled, state, steps):
    parts = [chunk_states(x, y, scaled, scale, rows) for rows in chunks_of(x)]
    for p, new in enumerate(block_states(parts, jnp.logical_not(is_low()), steps)):
        state[p] = new


def f_states(x, y, scale):
    length = x.shape[0]
    return pl.pallas_call(
        f_kernel,
        in_specs=[VMEM] * 3,
        out_specs=[VMEM] * 3,
        out_shape=[y_shape(length), STATE, steps_shape(length)],
        compiler_params=params(),
        name="f_states",
    )(in_vmem(x), in_vmem(y), in_vmem(scale))


def g_kernel(xa, ya, xb, yb, scale, fb, scaled_a, scaled_b, steps_a, steps_b, mixed, inner_b):
    low = is_low()
    inner = is_inner()
    parts = [chunk_states(xa, ya, scaled_a, scale, rows) for rows in chunks_of(xa)]
    for p, new in enumerate(block_states(parts, low, steps_a)):
        mixed[p] = jnp.where(inner, new, fb[p])
    parts = [chunk_states(xb, yb, scaled_b, scale, rows) for rows in chunks_of(xb)]
    for p, new in enumerate(block_states(parts, low, steps_b)):
        inner_b[p] = jnp.where(inner, new, 0.0)


def g_states(xa, ya, xb, yb, scale, fb):
    length = xa.shape[0]
    y, steps = y_shape(length), steps_shape(length)
    return pl.pallas_call(
        g_kernel,
        in_specs=[VMEM] * 6,
        out_specs=[VMEM] * 6,
        out_shape=[y, y, steps, steps, STATE, STATE],
        compiler_params=params(),
        name="g_states",
    )(*map(in_vmem, (xa, ya, xb, yb, scale, fb)))


def add_kernel(parts, a, b, *refs):
    outs = refs[-parts:]
    count = a.shape[0] // parts
    for i, out in enumerate(outs):
        for p in range(count):
            out[p] = a[i * count + p] + b[i * count + p]


def add(a, b, parts, after=()):
    shape = pltpu.VMEM((HALF // parts, XW, DV), F32)
    return pl.pallas_call(
        functools.partial(add_kernel, parts),
        in_specs=[VMEM] * (2 + len(after)),
        out_specs=[VMEM] * parts,
        out_shape=[shape] * parts,
        compiler_params=params(),
        name="add",
    )(a, b, *map(in_vmem, after))


def head_rows(x):
    lane = lax.broadcasted_iota(jnp.int32, x.shape, 1)
    zero = jnp.zeros_like(x)
    return jnp.concatenate([jnp.where(lane < DK, x, zero), jnp.where(lane >= DK, x, zero)], axis=0)


def head_blocks(y):
    zero = jnp.zeros_like(y[:, :DV])
    top = jnp.concatenate([y[:, :DV], zero], axis=1)
    return jnp.concatenate([top, jnp.concatenate([zero, y[:, DV:]], axis=1)], axis=0)


def state_blocks(state):
    row = lax.broadcasted_iota(jnp.int32, state.shape, 0)
    zero = jnp.zeros_like(state)
    both = jnp.concatenate([jnp.where(row < DK, state, zero), jnp.where(row >= DK, state, zero)], axis=1)
    return both.astype(BF16)


def turned(scores):
    return jnp.concatenate([scores[:, :CHUNK].T, scores[:, CHUNK:].T], axis=1)


def out_copies(staged, at, when_low, when_high, pair, width, sem):
    source = staged.at[:, pl.ds(at * width, width)]
    columns = pl.ds(pair * width, width)
    return [pltpu.make_async_copy(source, target.at[:, columns], sem.at[at]) for target in (when_low, when_high)]


def send(copies, low):
    @pl.when(low)
    def _():
        copies[0].start()

    @pl.when(jnp.logical_not(low))
    def _():
        copies[1].start()


def local_kernel(first, with_near, xf, yf, xg, yg, *refs):
    low = is_low()
    if with_near:
        steps, near, scale = refs[:3]
        att, qg, kg, vg, o2, o4, o1_out, o3_out, sem1, sem3 = refs[-10:]
    else:
        o1_out, o3_out, o2, o4 = refs[-4:]
    row = lax.broadcasted_iota(jnp.int32, (CHUNK, 2 * CHUNK), 0)
    col = lax.rem(lax.broadcasted_iota(jnp.int32, (CHUNK, 2 * CHUNK), 1), CHUNK)
    keep = jnp.where(low, row - col, col - row) >= 0
    chunks = chunks_of(xf)
    started = []
    for p in range(HALF):
        if with_near:
            base = jnp.where(is_inner(), near[p], 0.0)
        parts, scores = [], []
        for c, rows in enumerate(chunks):
            x1, y1, x2, y2 = xf[rows, xs(p)], yf[rows, ys(p)], xg[rows, xs(p)], yg[rows, ys(p)]
            blocks = state_blocks(base + steps[p, c]) if with_near else None
            parts.append((head_rows(x1), head_blocks(y1), x2, y2, blocks))
        for x1s, y1s, x2, y2, _ in parts:
            m = jnp.where(keep, dot(x2, x1s, NT), 0.0).astype(BF16)
            n = jnp.where(keep, dot(y2, y1s, NT), 0.0).astype(BF16)
            scores.append((m, n))
        for rows, (x1s, y1s, x2, y2, blocks), (m, n) in zip(chunks, parts, scores):
            o1, o3 = dot(m, y1s), dot(n, x1s)
            if with_near:
                o1 = (o1 + dot(x2, blocks)) * twice(scale[rows, :])
                o3 = o3 + dot(y2, blocks, NT)
            o1_out[rows, ys(p)] = o1.astype(o1_out.dtype)
            o3_out[rows, xs(p)] = o3.astype(o3_out.dtype)
            o2[rows, ys(p)] = dot(turned(m), head_blocks(y2))
            o4[rows, xs(p)] = dot(turned(n), head_rows(x2))
        if with_near:
            wide = out_copies(o1_out, p, att, vg, first + p, YW, sem1)
            narrow = out_copies(o3_out, p, qg, kg, first + p, XW, sem3)
            send(wide, low)
            send(narrow, low)
            started += [wide[0], narrow[0]]
    for copy in started:
        copy.wait()


def out_shapes(length):
    wide = jax.ShapeDtypeStruct((length, H * DV), BF16)
    narrow = jax.ShapeDtypeStruct((length, H * DK), BF16)
    return [wide, narrow, narrow, wide]


def out_scratch(length, count):
    return [
        pltpu.VMEM((length, count * YW), BF16),
        pltpu.VMEM((length, count * XW), BF16),
        pltpu.SemaphoreType.DMA((count,)),
        pltpu.SemaphoreType.DMA((count,)),
    ]


def local_terms(xf, yf, xg, yg):
    length = xf.shape[0]
    x, y = x_shape(length, F32), y_shape(length, F32)
    return pl.pallas_call(
        functools.partial(local_kernel, 0, False),
        in_specs=[VMEM] * 4,
        out_specs=[VMEM] * 4,
        out_shape=[y, x, y, x],
        compiler_params=params(),
        name="local",
    )(*map(in_vmem, (xf, yf, xg, yg)))


def local_near_terms(first, xf, yf, xg, yg, steps, near, scale, after):
    length = xf.shape[0]
    return pl.pallas_call(
        functools.partial(local_kernel, first, True),
        in_specs=[VMEM] * (7 + len(after)),
        out_specs=[HBM] * 4 + [VMEM] * 2,
        out_shape=out_shapes(length) + [y_shape(length, F32), x_shape(length, F32)],
        scratch_shapes=out_scratch(length, HALF),
        compiler_params=params(),
        name="local_near",
    )(*map(in_vmem, (xf, yf, xg, yg, steps)), near, in_vmem(scale), *map(in_vmem, after))


def cross(chunks, x, y, blocks, wide, narrow, at, pair, scale, wide_out, narrow_out, copies, low):
    a = [dot(x[rows, xs(at)], b) for rows, b in zip(chunks, blocks)]
    b = [dot(y[rows, ys(at)], b, NT) for rows, b in zip(chunks, blocks)]
    for rows, new in zip(chunks, a):
        wide_out[rows, ys(pair)] = ((wide[rows, ys(at)] + new) * twice(scale[rows, :])).astype(BF16)
    send(copies[0], low)
    for rows, new in zip(chunks, b):
        narrow_out[rows, xs(pair)] = (narrow[rows, xs(at)] + new).astype(BF16)
    send(copies[1], low)
    return [copies[0][0], copies[1][0]]


def finish_kernel(xf, yf, xg, yg, f_steps, g_steps, near, far1, far2, o1, o2, o3, o4, scale_low, scale_high, *refs):
    att, qg, kg, vg, o1_out, o3_out, sem1, sem3, o2_out, o4_out, sem2, sem4 = refs[-12:]
    low = is_low()
    inner = is_inner()
    chunks = chunks_of(xf)
    started = []
    for p in range(HALF):
        base = jnp.where(inner, near[p], 0.0)
        blocks = [state_blocks(base + f_steps[p, c]) for c in range(len(chunks))]
        copies = out_copies(o1_out, p, att, vg, p, YW, sem1), out_copies(o3_out, p, qg, kg, p, XW, sem3)
        started += cross(chunks, xg, yg, blocks, o1, o3, p, p, scale_low, o1_out, o3_out, copies, low)
        base = far1[p] + jnp.where(inner, 0.0, far2[p])
        blocks = [state_blocks(base + g_steps[p, c]) for c in range(len(chunks))]
        copies = out_copies(o2_out, p, vg, att, p, YW, sem2), out_copies(o4_out, p, kg, qg, p, XW, sem4)
        started += cross(chunks, xf, yf, blocks, o2, o4, p, p, scale_high, o2_out, o4_out, copies, low)
    for copy in started:
        copy.wait()


def finish_terms(xf, yf, xg, yg, f_steps, g_steps, near, far1, far2, o1, o2, o3, o4, scale_low, scale_high, outs):
    length = xf.shape[0]
    ins = [
        *map(in_vmem, (xf, yf, xg, yg, f_steps, g_steps)),
        near,
        far1,
        far2,
        *map(in_vmem, (o1, o2, o3, o4, scale_low, scale_high)),
    ]
    return pl.pallas_call(
        finish_kernel,
        in_specs=[VMEM] * len(ins) + [HBM] * 4,
        out_specs=[HBM] * 4,
        out_shape=out_shapes(length),
        input_output_aliases={len(ins) + i: i for i in range(4)},
        scratch_shapes=out_scratch(length, HALF) * 2,
        compiler_params=params(),
        name="finish",
    )(*ins, *outs)


def far_kernel(first, offset, count, xf, yf, steps, far1, far2, o2, o4, scale, *refs):
    att, qg, kg, vg, o2_out, o4_out, sem2, sem4 = refs[-8:]
    low = is_low()
    chunks = chunks_of(xf)
    started = []
    for i in range(count):
        p = offset + i
        base = far1[p] + far2[i]
        blocks = [state_blocks(base + steps[p, c]) for c in range(len(chunks))]
        pair = first + p
        copies = out_copies(o2_out, i, vg, att, pair, YW, sem2), out_copies(o4_out, i, kg, qg, pair, XW, sem4)
        started += cross(chunks, xf, yf, blocks, o2, o4, p, i, scale, o2_out, o4_out, copies, low)
    for copy in started:
        copy.wait()


def far_terms(first, offset, count, xf, yf, steps, far1, far2, o2, o4, scale, outs):
    length = xf.shape[0]
    ins = [*map(in_vmem, (xf, yf, steps)), far1, far2, *map(in_vmem, (o2, o4, scale))]
    return pl.pallas_call(
        functools.partial(far_kernel, first, offset, count),
        in_specs=[VMEM] * 8 + [HBM] * 4,
        out_specs=[HBM] * 4,
        out_shape=out_shapes(length),
        input_output_aliases={8 + i: i for i in range(4)},
        scratch_shapes=out_scratch(length, count),
        compiler_params=params(),
        name="far",
    )(*ins, *outs)


def scan_sum(state, size, sign):
    def moved(array, step):
        return lax.ppermute(array, "ctx", [(i, i + sign * step) for i in range(size) if 0 <= i + sign * step < size])

    total, step = moved(state, 1), 1
    while step < size:
        total, step = total + moved(total, step), 2 * step
    return total


def local(queries, keys, values, out_grad):
    size = lax.axis_size("ctx")
    xfa, yfa, xfb, yfb, xga, yga, xgb, ygb, scale_low, scale_high, fa, fa_steps = load(
        *map(in_hbm, (queries, keys, values, out_grad))
    )
    swap_x = [(0, 1), (1, 0), (2, 3), (3, 2)]
    swap_y = [(0, 2), (2, 0), (1, 3), (3, 1)]
    if size == 4:
        got_xa = lax.ppermute(fa, "ctx", swap_x)
    yfb, fb, fb_steps = f_states(xfb, yfb, scale_high)
    if size == 4:
        got_y1 = lax.ppermute(fb, "ctx", swap_y)
    yga, ygb, ga_steps, gb_steps, mixed, inner_b = g_states(xga, yga, xgb, ygb, scale_low, fb)
    if size == 4:
        got_xb = lax.ppermute(mixed, "ctx", swap_x)
    o1a, o3a, o2a, o4a = local_terms(xfa, yfa, xga, yga)
    if size == 4:
        (sum_a,) = add(fa, got_xa, 1, [o4a])
        got_y2 = lax.ppermute(sum_a, "ctx", swap_y)
        sums = add(got_y1, inner_b, SPLIT, [sum_a])
        far_last = [lax.ppermute(s, "ctx", swap_x) for s in sums]
        near_a, near_b, token = got_xa, got_xb, list(sums)
        far_a, far_b = (got_y2, got_xb), got_y1
    else:
        near_a, near_b, token = scan_sum(fa, size, 1), scan_sum(fb, size, 1), []
        far_a, far_b = (scan_sum(mixed, size, -1), mixed), scan_sum(inner_b, size, -1)
        far_last = [jnp.zeros((HALF // SPLIT, XW, DV), F32)] * SPLIT
    *outs, o2b, o4b = local_near_terms(HALF, xfb, yfb, xgb, ygb, fb_steps, near_b, scale_low, token)
    outs = finish_terms(
        xfa, yfa, xga, yga, fa_steps, ga_steps, near_a, *far_a, o1a, o2a, o3a, o4a, scale_low, scale_high, outs
    )
    count = HALF // SPLIT
    for i in range(SPLIT):
        outs = far_terms(HALF, i * count, count, xfb, yfb, gb_steps, far_b, far_last[i], o2b, o4b, scale_high, outs)
    return tuple(outs)


def solution(mesh):
    spec = P(("batch", "ctx"), None)
    return jax.shard_map(local, mesh=mesh, in_specs=(spec,) * 4, out_specs=(spec,) * 4, check_vma=False)
```

```python
import functools
import typing

import jax
import jax.numpy as jnp
from jax import lax
from jax.experimental import pallas as pl
from jax.experimental.pallas import tpu as pltpu
from jax.sharding import PartitionSpec as P


H = 16
DK = 64
DV = 128
PAIRS = H // 2
HALF = PAIRS // 2
XW = 2 * DK
YW = 2 * DV
CHUNK = 128
CUTS = ((0, 3), (3, 4))
VMEM_LIMIT = 12 * 1024 * 1024

NN = (((1,), (0,)), ((), ()))
NT = (((1,), (1,)), ((), ()))
TN = (((0,), (0,)), ((), ()))
F32 = jnp.float32
BF16 = jnp.bfloat16

HBM = pl.BlockSpec(memory_space=pltpu.HBM)
VMEM = pl.BlockSpec(memory_space=pltpu.VMEM)


def dot(a, b, dims=NN):
    return lax.dot_general(a, b, dims, preferred_element_type=F32)


def is_low():
    size = lax.axis_size("ctx")
    return lax.axis_index("ctx") < (size // 2 if size == 4 else size)


def is_inner():
    at = lax.axis_index("ctx")
    return (at == 1) | (at == 2) if lax.axis_size("ctx") == 4 else at >= 0


def in_vmem(array):
    return pltpu.with_memory_space_constraint(array, pltpu.VMEM)


def in_hbm(array):
    return pltpu.with_memory_space_constraint(array, pltpu.HBM)


def x_shape(length, dtype=BF16):
    return pltpu.VMEM((length, HALF * XW), dtype)


def y_shape(length, dtype=BF16):
    return pltpu.VMEM((length, HALF * YW), dtype)


STATE = pltpu.VMEM((HALF, XW, DV), F32)


def steps_shape(length):
    return pltpu.VMEM((HALF, length // CHUNK, XW, DV), F32)


def params():
    return pltpu.CompilerParams(vmem_limit_bytes=VMEM_LIMIT)


def diagonal(square):
    return jnp.concatenate([square[:DK, :DV], square[DK:, DV:]], axis=0)


def xs(p):
    return slice(p * XW, (p + 1) * XW)


def ys(p):
    return slice(p * YW, (p + 1) * YW)


def chunks_of(array):
    return [slice(c, c + CHUNK) for c in range(0, array.shape[0], CHUNK)]


def twice(scale):
    return jnp.concatenate([scale, scale], axis=1)


def chunk_states(x, y, scaled, scale, rows):
    s = twice(scale[rows, :])
    states = []
    for p in range(HALF):
        new = (y[rows, ys(p)].astype(F32) * s).astype(BF16)
        scaled[rows, ys(p)] = new
        states.append(diagonal(dot(x[rows, xs(p)], new, TN)))
    return states


def block_states(parts, backward, steps):
    count = len(parts)
    states = []
    for p in range(HALF):
        zero = jnp.zeros_like(parts[0][p])
        before, after = [zero], [zero]
        for c in range(count - 1):
            before.append(before[-1] + parts[c][p])
            after.append(after[-1] + parts[count - 1 - c][p])
        for c in range(count):
            steps[p, c] = jnp.where(backward, after[count - 1 - c], before[c])
        states.append(before[-1] + parts[-1][p])
    return states


def half_copies(a, b, x, y, half, sems):
    wide, narrow = pl.ds(half * HALF * YW, HALF * YW), pl.ds(half * HALF * XW, HALF * XW)
    return [
        (
            pltpu.make_async_copy(a.at[rows, narrow], x.at[rows, :], sems.at[0, c]),
            pltpu.make_async_copy(b.at[rows, wide], y.at[rows, :], sems.at[1, c]),
        )
        for c, rows in enumerate(chunks_of(a))
    ]


def start_all(chunks):
    for pair in chunks:
        for copy in pair:
            copy.start()


def arrived_states(copies, x, y, scaled, scale, state, steps):
    parts = []
    for rows, pair in zip(chunks_of(x), copies):
        for copy in pair:
            copy.wait()
        parts.append(chunk_states(x, y, scaled, scale, rows))
    for p, new in enumerate(block_states(parts, jnp.logical_not(is_low()), steps)):
        state[p] = new


def load_kernel(q, k, v, do, x, y, scale_low, scale_high, state, steps, raw, sems):
    low = is_low()
    length = q.shape[0]

    @pl.when(low)
    def _():
        start_all(half_copies(k, v, x, raw, 0, sems))

    @pl.when(jnp.logical_not(low))
    def _():
        start_all(half_copies(q, do, x, raw, 0, sems))

    at = lax.axis_index("ctx") * length + lax.broadcasted_iota(jnp.int32, (length, DV), 0)
    scale = 1.0 / jnp.sqrt(DK * (at.astype(F32) + 1.0))
    scale_low[...] = jnp.where(low, scale, 1.0)
    scale_high[...] = jnp.where(low, 1.0, scale)
    arrived_states(half_copies(k, v, x, raw, 0, sems), x, raw, y, scale_high, state, steps)


def load(q, k, v, do):
    length = q.shape[0]
    scale = pltpu.VMEM((length, DV), F32)
    return pl.pallas_call(
        load_kernel,
        in_specs=[HBM] * 4,
        out_specs=[VMEM] * 6,
        out_shape=[x_shape(length), y_shape(length), scale, scale, STATE, steps_shape(length)],
        scratch_shapes=[y_shape(length), pltpu.SemaphoreType.DMA((2, length // CHUNK))],
        compiler_params=params(),
        name="load",
    )(q, k, v, do)


def rest_kernel(q, k, v, do, scale, xfb, yfb, xga, yga, xgb, ygb, state, steps, raw, sems):
    def start(f, g):
        start_all(half_copies(*f, xfb, raw, 1, sems.at[0]))
        start_all(half_copies(*g, xga, yga, 0, sems.at[1]))
        start_all(half_copies(*g, xgb, ygb, 1, sems.at[2]))

    low = is_low()

    @pl.when(low)
    def _():
        start((k, v), (q, do))

    @pl.when(jnp.logical_not(low))
    def _():
        start((q, do), (k, v))

    arrived_states(half_copies(k, v, xfb, raw, 1, sems.at[0]), xfb, raw, yfb, scale, state, steps)
    for x, y, half in ((xga, yga, 0), (xgb, ygb, 1)):
        for pair in half_copies(k, v, x, y, half, sems.at[half + 1]):
            for copy in pair:
                copy.wait()


def rest(q, k, v, do, scale):
    length = q.shape[0]
    x, y = x_shape(length), y_shape(length)
    return pl.pallas_call(
        rest_kernel,
        in_specs=[HBM] * 4 + [VMEM],
        out_specs=[VMEM] * 8,
        out_shape=[x, y, x, y, x, y, STATE, steps_shape(length)],
        scratch_shapes=[y, pltpu.SemaphoreType.DMA((3, 2, length // CHUNK))],
        compiler_params=params(),
        name="rest",
    )(q, k, v, do, in_vmem(scale))


def g_kernel(xa, ya, xb, yb, scale, fb, scaled_a, scaled_b, steps_a, steps_b, mixed, inner_b):
    low = is_low()
    inner = is_inner()
    parts = [chunk_states(xa, ya, scaled_a, scale, rows) for rows in chunks_of(xa)]
    for p, new in enumerate(block_states(parts, low, steps_a)):
        mixed[p] = jnp.where(inner, new, fb[p])
    parts = [chunk_states(xb, yb, scaled_b, scale, rows) for rows in chunks_of(xb)]
    for p, new in enumerate(block_states(parts, low, steps_b)):
        inner_b[p] = jnp.where(inner, new, 0.0)


def g_states(xa, ya, xb, yb, scale, fb):
    length = xa.shape[0]
    y, steps = y_shape(length), steps_shape(length)
    return pl.pallas_call(
        g_kernel,
        in_specs=[VMEM] * 6,
        out_specs=[VMEM] * 6,
        out_shape=[y, y, steps, steps, STATE, STATE],
        compiler_params=params(),
        name="g_states",
    )(*map(in_vmem, (xa, ya, xb, yb, scale, fb)))


def add_kernel(cuts, a, b, *refs):
    for (start, stop), out in zip(cuts, refs[-len(cuts) :]):
        for p in range(start, stop):
            out[p - start] = a[p] + b[p]


def add(a, b, cuts, after=()):
    return pl.pallas_call(
        functools.partial(add_kernel, cuts),
        in_specs=[VMEM] * (2 + len(after)),
        out_specs=[VMEM] * len(cuts),
        out_shape=[pltpu.VMEM((stop - start, XW, DV), F32) for start, stop in cuts],
        compiler_params=params(),
        name="add",
    )(a, b, *map(in_vmem, after))


def head_rows(x):
    lane = lax.broadcasted_iota(jnp.int32, x.shape, 1)
    zero = jnp.zeros_like(x)
    return jnp.concatenate([jnp.where(lane < DK, x, zero), jnp.where(lane >= DK, x, zero)], axis=0)


def head_blocks(y):
    zero = jnp.zeros_like(y[:, :DV])
    top = jnp.concatenate([y[:, :DV], zero], axis=1)
    return jnp.concatenate([top, jnp.concatenate([zero, y[:, DV:]], axis=1)], axis=0)


def state_blocks(state):
    row = lax.broadcasted_iota(jnp.int32, state.shape, 0)
    zero = jnp.zeros_like(state)
    both = jnp.concatenate([jnp.where(row < DK, state, zero), jnp.where(row >= DK, state, zero)], axis=1)
    return both.astype(BF16)


def turned(scores):
    return jnp.concatenate([scores[:, :CHUNK].T, scores[:, CHUNK:].T], axis=1)


def out_copies(staged, at, when_low, when_high, pair, width, sem):
    source = staged.at[:, pl.ds(at * width, width)]
    columns = pl.ds(pair * width, width)
    return [pltpu.make_async_copy(source, target.at[:, columns], sem.at[at]) for target in (when_low, when_high)]


def send(copies, low):
    @pl.when(low)
    def _():
        copies[0].start()

    @pl.when(jnp.logical_not(low))
    def _():
        copies[1].start()


def local_kernel(start, stop, xf, yf, xg, yg, *refs):
    low = is_low()
    o1, o3, o2, o4 = refs[-4:]
    row = lax.broadcasted_iota(jnp.int32, (CHUNK, 2 * CHUNK), 0)
    col = lax.rem(lax.broadcasted_iota(jnp.int32, (CHUNK, 2 * CHUNK), 1), CHUNK)
    keep = jnp.where(low, row - col, col - row) >= 0
    chunks = chunks_of(xf)
    for p in range(start, stop):
        parts, scores = [], []
        for rows in chunks:
            x1, y1, x2, y2 = xf[rows, xs(p)], yf[rows, ys(p)], xg[rows, xs(p)], yg[rows, ys(p)]
            parts.append((head_rows(x1), head_blocks(y1), x2, y2))
        for x1s, y1s, x2, y2 in parts:
            m = jnp.where(keep, dot(x2, x1s, NT), 0.0).astype(BF16)
            n = jnp.where(keep, dot(y2, y1s, NT), 0.0).astype(BF16)
            scores.append((m, n))
        wide, narrow = ys(p - start), xs(p - start)
        for rows, (x1s, y1s, x2, y2), (m, n) in zip(chunks, parts, scores):
            o1[rows, wide] = dot(m, y1s)
            o3[rows, narrow] = dot(n, x1s)
            o2[rows, wide] = dot(turned(m), head_blocks(y2))
            o4[rows, narrow] = dot(turned(n), head_rows(x2))


def local_terms(start, stop, arrays, after=()):
    length = arrays[0].shape[0]
    wide = pltpu.VMEM((length, (stop - start) * YW), F32)
    narrow = pltpu.VMEM((length, (stop - start) * XW), F32)
    return pl.pallas_call(
        functools.partial(local_kernel, start, stop),
        in_specs=[VMEM] * (4 + len(after)),
        out_specs=[VMEM] * 4,
        out_shape=[wide, narrow, wide, narrow],
        compiler_params=params(),
        name="local",
    )(*map(in_vmem, (*arrays, *after)))


class Job(typing.NamedTuple):
    arrays: tuple
    at: int
    part: int
    second: int
    pair: int


def cross_kernel(places, near, scale_at, *refs):
    att, qg, kg, vg, wide_out, narrow_out, wide_sem, narrow_sem = refs[-8:]
    low = is_low()
    inner = is_inner()
    scale = refs[scale_at]
    started = []
    for i, (where, at, part, second, pair) in enumerate(places):
        x, y, steps, wide, narrow, *terms = [refs[w] for w in where]
        base = terms[0][at]
        if near:
            base = jnp.where(inner, base, 0.0)
        elif len(terms) > 1:
            base = base + (jnp.where(inner, 0.0, terms[1][at]) if second < 0 else terms[1][second])
        chunks = chunks_of(x)
        blocks = [state_blocks(base + steps[at, c]) for c in range(len(chunks))]
        a = [dot(x[rows, xs(at)], b) for rows, b in zip(chunks, blocks)]
        b = [dot(y[rows, ys(at)], b, NT) for rows, b in zip(chunks, blocks)]
        targets = (att, vg, qg, kg) if near else (vg, att, kg, qg)
        to_wide = out_copies(wide_out, i, targets[0], targets[1], pair, YW, wide_sem)
        to_narrow = out_copies(narrow_out, i, targets[2], targets[3], pair, XW, narrow_sem)
        for rows, new in zip(chunks, a):
            wide_out[rows, ys(i)] = ((wide[rows, ys(part)] + new) * twice(scale[rows, :])).astype(BF16)
        send(to_wide, low)
        for rows, new in zip(chunks, b):
            narrow_out[rows, xs(i)] = (narrow[rows, xs(part)] + new).astype(BF16)
        send(to_narrow, low)
        started += [to_wide[0], to_narrow[0]]
    for copy in started:
        copy.wait()


def cross_terms(jobs, near, scale, outs, received):
    arrays = []

    def place(array):
        for i, other in enumerate(arrays):
            if other is array:
                return i
        arrays.append(array)
        return len(arrays) - 1

    scale_at = place(scale)
    places = [(tuple(map(place, job.arrays)), *job[1:]) for job in jobs]
    length = scale.shape[0]
    ins = [a if any(a is r for r in received) else in_vmem(a) for a in arrays]
    count = len(jobs)
    return pl.pallas_call(
        functools.partial(cross_kernel, places, near, scale_at),
        in_specs=[VMEM] * len(ins) + [HBM] * len(outs),
        out_specs=[HBM] * 4,
        out_shape=[
            jax.ShapeDtypeStruct((length, H * DV), BF16),
            jax.ShapeDtypeStruct((length, H * DK), BF16),
            jax.ShapeDtypeStruct((length, H * DK), BF16),
            jax.ShapeDtypeStruct((length, H * DV), BF16),
        ],
        input_output_aliases={len(ins) + i: i for i in range(len(outs))},
        scratch_shapes=[
            pltpu.VMEM((length, count * YW), BF16),
            pltpu.VMEM((length, count * XW), BF16),
            pltpu.SemaphoreType.DMA((count,)),
            pltpu.SemaphoreType.DMA((count,)),
        ],
        compiler_params=params(),
        name="near" if near else "far",
    )(*ins, *outs)


def scan_sum(state, size, sign):
    def moved(array, step):
        return lax.ppermute(array, "ctx", [(i, i + sign * step) for i in range(size) if 0 <= i + sign * step < size])

    total, step = moved(state, 1), 1
    while step < size:
        total, step = total + moved(total, step), 2 * step
    return total


def local(queries, keys, values, out_grad):
    size = lax.axis_size("ctx")
    args = list(map(in_hbm, (queries, keys, values, out_grad)))
    swap_x = [(0, 1), (1, 0), (2, 3), (3, 2)]
    swap_y = [(0, 2), (2, 0), (1, 3), (3, 1)]
    xfa, yfa, scale_low, scale_high, fa, fa_steps = load(*args)
    if size == 4:
        got_xa = lax.ppermute(fa, "ctx", swap_x)
    xfb, yfb, xga, yga, xgb, ygb, fb, fb_steps = rest(*args, scale_high)
    if size == 4:
        got_y1 = lax.ppermute(fb, "ctx", swap_y)
    yga, ygb, ga_steps, gb_steps, mixed, inner_b = g_states(xga, yga, xgb, ygb, scale_low, fb)
    if size == 4:
        got_xb = lax.ppermute(mixed, "ctx", swap_x)
    half_a, half_b = (xfa, yfa, xga, yga), (xfb, yfb, xgb, ygb)
    part_a = local_terms(0, HALF, half_a)
    if size == 4:
        (sum_a,) = add(fa, got_xa, [(0, HALF)], [part_a[0]])
        got_y2 = lax.ppermute(sum_a, "ctx", swap_y)
        after = [sum_a]
    else:
        after = []
    parts_b = [local_terms(*CUTS[0], half_b, after)]
    if size == 4:
        sums = add(got_y1, inner_b, CUTS, [parts_b[0][0]])
        far_last = [lax.ppermute(s, "ctx", swap_x) for s in sums]
        near_a, near_b = got_xa, got_xb
        far_a, far_b = (got_y2, got_xb), got_y1
        after = list(sums)
    else:
        near_a, near_b = scan_sum(fa, size, 1), scan_sum(fb, size, 1)
        far_a, far_b = (scan_sum(mixed, size, -1),), scan_sum(inner_b, size, -1)
    parts_b += [local_terms(*cut, half_b, after) for cut in CUTS[1:]]
    received = (near_a, near_b, *far_a, far_b)
    places = [(cut, p) for cut in range(len(CUTS)) for p in range(*CUTS[cut])]
    jobs = [Job((xga, yga, fa_steps, part_a[0], part_a[1], near_a), p, p, 0, p) for p in range(HALF)]
    for cut, p in places:
        arrays = (xgb, ygb, fb_steps, parts_b[cut][0], parts_b[cut][1], near_b)
        jobs.append(Job(arrays, p, p - CUTS[cut][0], 0, HALF + p))
    outs = cross_terms(jobs, True, scale_low, [], received)
    jobs = [Job((xfa, yfa, ga_steps, part_a[2], part_a[3], *far_a), p, p, -1, p) for p in range(HALF)]
    outs = cross_terms(jobs, False, scale_high, outs, received)
    for cut, (start, stop) in enumerate(CUTS):
        last = (far_last[cut],) if size == 4 else ()
        arrays = (xfb, yfb, gb_steps, parts_b[cut][2], parts_b[cut][3], far_b, *last)
        jobs = [Job(arrays, p, p - start, p - start, HALF + p) for p in range(start, stop)]
        outs = cross_terms(jobs, False, scale_high, outs, (*received, *last))
    return tuple(outs)


def solution(mesh):
    spec = P(("batch", "ctx"), None)
    return jax.shard_map(local, mesh=mesh, in_specs=(spec,) * 4, out_specs=(spec,) * 4, check_vma=False)
```

```python
import functools
import typing

import jax
import jax.numpy as jnp
from jax import lax
from jax.experimental import pallas as pl
from jax.experimental.pallas import tpu as pltpu
from jax.sharding import PartitionSpec as P


H = 16
DK = 64
DV = 128
PAIRS = H // 2
HALF = PAIRS // 2
XW = 2 * DK
YW = 2 * DV
CHUNK = 128
CUTS = ((0, 4),)
VMEM_LIMIT = 12 * 1024 * 1024

NN = (((1,), (0,)), ((), ()))
NT = (((1,), (1,)), ((), ()))
TN = (((0,), (0,)), ((), ()))
F32 = jnp.float32
BF16 = jnp.bfloat16

HBM = pl.BlockSpec(memory_space=pltpu.HBM)
VMEM = pl.BlockSpec(memory_space=pltpu.VMEM)


def dot(a, b, dims=NN):
    return lax.dot_general(a, b, dims, preferred_element_type=F32)


def is_low():
    size = lax.axis_size("ctx")
    return lax.axis_index("ctx") < (size // 2 if size == 4 else size)


def is_inner():
    at = lax.axis_index("ctx")
    return (at == 1) | (at == 2) if lax.axis_size("ctx") == 4 else at >= 0


def in_vmem(array):
    return pltpu.with_memory_space_constraint(array, pltpu.VMEM)


def in_hbm(array):
    return pltpu.with_memory_space_constraint(array, pltpu.HBM)


def x_shape(length, dtype=BF16):
    return pltpu.VMEM((length, HALF * XW), dtype)


def y_shape(length, dtype=BF16):
    return pltpu.VMEM((length, HALF * YW), dtype)


STATE = pltpu.VMEM((HALF, XW, DV), F32)


def steps_shape(length):
    return pltpu.VMEM((HALF, length // CHUNK, XW, DV), F32)


def params():
    return pltpu.CompilerParams(vmem_limit_bytes=VMEM_LIMIT)


def diagonal(square):
    return jnp.concatenate([square[:DK, :DV], square[DK:, DV:]], axis=0)


def xs(p):
    return slice(p * XW, (p + 1) * XW)


def ys(p):
    return slice(p * YW, (p + 1) * YW)


def chunks_of(array):
    return [slice(c, c + CHUNK) for c in range(0, array.shape[0], CHUNK)]


def twice(scale):
    return jnp.concatenate([scale, scale], axis=1)


def chunk_states(x, y, scaled, scale, rows, half=0, kept=None):
    s = twice(scale[rows, :])
    states = []
    for p in range(HALF):
        old = x[rows, xs(half * HALF + p)]
        if kept is not None:
            kept[rows, xs(p)] = old
        new = (y[rows, ys(half * HALF + p)].astype(F32) * s).astype(BF16)
        scaled[rows, ys(p)] = new
        states.append(diagonal(dot(old, new, TN)))
    return states


def block_states(parts, backward, steps):
    count = len(parts)
    states = []
    for p in range(HALF):
        zero = jnp.zeros_like(parts[0][p])
        before, after = [zero], [zero]
        for c in range(count - 1):
            before.append(before[-1] + parts[c][p])
            after.append(after[-1] + parts[count - 1 - c][p])
        for c in range(count):
            steps[p, c] = jnp.where(backward, after[count - 1 - c], before[c])
        states.append(before[-1] + parts[-1][p])
    return states


def half_copies(a, b, x, y, half, sems):
    wide, narrow = pl.ds(half * HALF * YW, HALF * YW), pl.ds(half * HALF * XW, HALF * XW)
    return [
        (
            pltpu.make_async_copy(a.at[rows, narrow], x.at[rows, :], sems.at[0, c]),
            pltpu.make_async_copy(b.at[rows, wide], y.at[rows, :], sems.at[1, c]),
        )
        for c, rows in enumerate(chunks_of(a))
    ]


def start_all(chunks):
    for pair in chunks:
        for copy in pair:
            copy.start()


def arrived_states(copies, x, y, scaled, scale, state, steps):
    parts = []
    for rows, pair in zip(chunks_of(x), copies):
        for copy in pair:
            copy.wait()
        parts.append(chunk_states(x, y, scaled, scale, rows))
    for p, new in enumerate(block_states(parts, jnp.logical_not(is_low()), steps)):
        state[p] = new


def load_kernel(q, k, v, do, x, y, scale_low, scale_high, state, steps, raw, sems):
    low = is_low()
    length = q.shape[0]

    @pl.when(low)
    def _():
        start_all(half_copies(k, v, x, raw, 0, sems))

    @pl.when(jnp.logical_not(low))
    def _():
        start_all(half_copies(q, do, x, raw, 0, sems))

    at = lax.axis_index("ctx") * length + lax.broadcasted_iota(jnp.int32, (length, DV), 0)
    scale = 1.0 / jnp.sqrt(DK * (at.astype(F32) + 1.0))
    scale_low[...] = jnp.where(low, scale, 1.0)
    scale_high[...] = jnp.where(low, 1.0, scale)
    arrived_states(half_copies(k, v, x, raw, 0, sems), x, raw, y, scale_high, state, steps)


def load(q, k, v, do):
    length = q.shape[0]
    scale = pltpu.VMEM((length, DV), F32)
    return pl.pallas_call(
        load_kernel,
        in_specs=[HBM] * 4,
        out_specs=[VMEM] * 6,
        out_shape=[x_shape(length), y_shape(length), scale, scale, STATE, steps_shape(length)],
        scratch_shapes=[y_shape(length), pltpu.SemaphoreType.DMA((2, length // CHUNK))],
        compiler_params=params(),
        name="load",
    )(q, k, v, do)


def either(low, work, kv, qd):
    @pl.when(low)
    def _():
        work(*kv)

    @pl.when(jnp.logical_not(low))
    def _():
        work(*qd)


def f_kernel(q, k, v, do, scale, x, y, state, steps):
    low = is_low()

    def work(a, b):
        parts = [chunk_states(a, b, y, scale, rows, 1, x) for rows in chunks_of(x)]
        for p, new in enumerate(block_states(parts, jnp.logical_not(low), steps)):
            state[p] = new

    either(low, work, (k, v), (q, do))


def f_states(q, k, v, do, scale):
    length = q.shape[0]
    return pl.pallas_call(
        f_kernel,
        in_specs=[VMEM] * 5,
        out_specs=[VMEM] * 4,
        out_shape=[x_shape(length), y_shape(length), STATE, steps_shape(length)],
        compiler_params=params(),
        name="f_states",
    )(*map(in_vmem, (q, k, v, do, scale)))


def g_kernel(q, k, v, do, scale, fb, xa, ya, xb, yb, steps_a, steps_b, mixed, inner_b):
    low = is_low()
    inner = is_inner()

    def work(a, b):
        parts = [chunk_states(a, b, ya, scale, rows, 0, xa) for rows in chunks_of(xa)]
        for p, new in enumerate(block_states(parts, low, steps_a)):
            mixed[p] = jnp.where(inner, new, fb[p])
        parts = [chunk_states(a, b, yb, scale, rows, 1, xb) for rows in chunks_of(xb)]
        for p, new in enumerate(block_states(parts, low, steps_b)):
            inner_b[p] = jnp.where(inner, new, 0.0)

    either(low, work, (q, do), (k, v))


def g_states(q, k, v, do, scale, fb):
    length = q.shape[0]
    x, y, steps = x_shape(length), y_shape(length), steps_shape(length)
    return pl.pallas_call(
        g_kernel,
        in_specs=[VMEM] * 6,
        out_specs=[VMEM] * 8,
        out_shape=[x, y, x, y, steps, steps, STATE, STATE],
        compiler_params=params(),
        name="g_states",
    )(*map(in_vmem, (q, k, v, do, scale, fb)))


def add_kernel(cuts, a, b, *refs):
    for (start, stop), out in zip(cuts, refs[-len(cuts) :]):
        for p in range(start, stop):
            out[p - start] = a[p] + b[p]


def add(a, b, cuts, after=()):
    return pl.pallas_call(
        functools.partial(add_kernel, cuts),
        in_specs=[VMEM] * (2 + len(after)),
        out_specs=[VMEM] * len(cuts),
        out_shape=[pltpu.VMEM((stop - start, XW, DV), F32) for start, stop in cuts],
        compiler_params=params(),
        name="add",
    )(a, b, *map(in_vmem, after))


def head_rows(x):
    lane = lax.broadcasted_iota(jnp.int32, x.shape, 1)
    zero = jnp.zeros_like(x)
    return jnp.concatenate([jnp.where(lane < DK, x, zero), jnp.where(lane >= DK, x, zero)], axis=0)


def head_blocks(y):
    zero = jnp.zeros_like(y[:, :DV])
    top = jnp.concatenate([y[:, :DV], zero], axis=1)
    return jnp.concatenate([top, jnp.concatenate([zero, y[:, DV:]], axis=1)], axis=0)


def state_blocks(state):
    row = lax.broadcasted_iota(jnp.int32, state.shape, 0)
    zero = jnp.zeros_like(state)
    both = jnp.concatenate([jnp.where(row < DK, state, zero), jnp.where(row >= DK, state, zero)], axis=1)
    return both.astype(BF16)


def turned(scores):
    return jnp.concatenate([scores[:, :CHUNK].T, scores[:, CHUNK:].T], axis=1)


def out_copies(staged, at, when_low, when_high, pair, width, sem):
    source = staged.at[:, pl.ds(at * width, width)]
    columns = pl.ds(pair * width, width)
    return [pltpu.make_async_copy(source, target.at[:, columns], sem.at[at]) for target in (when_low, when_high)]


def send(copies, low):
    @pl.when(low)
    def _():
        copies[0].start()

    @pl.when(jnp.logical_not(low))
    def _():
        copies[1].start()


def local_kernel(xf, yf, xg, yg, o1, o3, o2, o4):
    low = is_low()
    row = lax.broadcasted_iota(jnp.int32, (CHUNK, 2 * CHUNK), 0)
    col = lax.rem(lax.broadcasted_iota(jnp.int32, (CHUNK, 2 * CHUNK), 1), CHUNK)
    keep = jnp.where(low, row - col, col - row) >= 0
    chunks = chunks_of(xf)
    for p in range(HALF):
        parts, scores = [], []
        for rows in chunks:
            x1, y1, x2, y2 = xf[rows, xs(p)], yf[rows, ys(p)], xg[rows, xs(p)], yg[rows, ys(p)]
            parts.append((head_rows(x1), head_blocks(y1), x2, y2))
        for x1s, y1s, x2, y2 in parts:
            m = jnp.where(keep, dot(x2, x1s, NT), 0.0).astype(BF16)
            n = jnp.where(keep, dot(y2, y1s, NT), 0.0).astype(BF16)
            scores.append((m, n))
        for rows, (x1s, y1s, x2, y2), (m, n) in zip(chunks, parts, scores):
            o1[rows, ys(p)] = dot(m, y1s)
            o3[rows, xs(p)] = dot(n, x1s)
            o2[rows, ys(p)] = dot(turned(m), head_blocks(y2))
            o4[rows, xs(p)] = dot(turned(n), head_rows(x2))


def local_terms(arrays):
    length = arrays[0].shape[0]
    x, y = x_shape(length, F32), y_shape(length, F32)
    return pl.pallas_call(
        local_kernel,
        in_specs=[VMEM] * 4,
        out_specs=[VMEM] * 4,
        out_shape=[y, x, y, x],
        compiler_params=params(),
        name="local",
    )(*map(in_vmem, arrays))


class Job(typing.NamedTuple):
    arrays: tuple
    at: int
    second: int
    pair: int


def cross_kernel(places, near, scale_at, *refs):
    att, qg, kg, vg, wide_out, narrow_out, wide_sem, narrow_sem = refs[-8:]
    low = is_low()
    inner = is_inner()
    scale = refs[scale_at]
    started = []
    for i, (where, at, second, pair) in enumerate(places):
        x, y, steps, wide, narrow, *terms = [refs[w] for w in where]
        base = terms[0][at]
        if near:
            base = jnp.where(inner, base, 0.0)
        elif len(terms) > 1:
            base = base + (jnp.where(inner, 0.0, terms[1][at]) if second < 0 else terms[1][second])
        chunks = chunks_of(x)
        blocks = [state_blocks(base + steps[at, c]) for c in range(len(chunks))]
        a = [dot(x[rows, xs(at)], b) for rows, b in zip(chunks, blocks)]
        b = [dot(y[rows, ys(at)], b, NT) for rows, b in zip(chunks, blocks)]
        targets = (att, vg, qg, kg) if near else (vg, att, kg, qg)
        to_wide = out_copies(wide_out, i, targets[0], targets[1], pair, YW, wide_sem)
        to_narrow = out_copies(narrow_out, i, targets[2], targets[3], pair, XW, narrow_sem)
        for rows, new in zip(chunks, a):
            wide_out[rows, ys(i)] = ((wide[rows, ys(at)] + new) * twice(scale[rows, :])).astype(BF16)
        send(to_wide, low)
        for rows, new in zip(chunks, b):
            narrow_out[rows, xs(i)] = (narrow[rows, xs(at)] + new).astype(BF16)
        send(to_narrow, low)
        started += [to_wide[0], to_narrow[0]]
    for copy in started:
        copy.wait()


def cross_terms(jobs, near, scale, outs, received, after=()):
    arrays = []

    def place(array):
        for i, other in enumerate(arrays):
            if other is array:
                return i
        arrays.append(array)
        return len(arrays) - 1

    scale_at = place(scale)
    places = [(tuple(map(place, job.arrays)), *job[1:]) for job in jobs]
    length = scale.shape[0]
    ins = [a if any(a is r for r in received) else in_vmem(a) for a in arrays]
    count = len(jobs)
    return pl.pallas_call(
        functools.partial(cross_kernel, places, near, scale_at),
        in_specs=[VMEM] * len(ins) + [HBM] * len(outs) + [VMEM] * len(after),
        out_specs=[HBM] * 4,
        out_shape=[
            jax.ShapeDtypeStruct((length, H * DV), BF16),
            jax.ShapeDtypeStruct((length, H * DK), BF16),
            jax.ShapeDtypeStruct((length, H * DK), BF16),
            jax.ShapeDtypeStruct((length, H * DV), BF16),
        ],
        input_output_aliases={len(ins) + i: i for i in range(len(outs))},
        scratch_shapes=[
            pltpu.VMEM((length, count * YW), BF16),
            pltpu.VMEM((length, count * XW), BF16),
            pltpu.SemaphoreType.DMA((count,)),
            pltpu.SemaphoreType.DMA((count,)),
        ],
        compiler_params=params(),
        name="near" if near else "far",
    )(*ins, *outs, *map(in_vmem, after))


def scan_sum(state, size, sign):
    def moved(array, step):
        return lax.ppermute(array, "ctx", [(i, i + sign * step) for i in range(size) if 0 <= i + sign * step < size])

    total, step = moved(state, 1), 1
    while step < size:
        total, step = total + moved(total, step), 2 * step
    return total


def local(queries, keys, values, out_grad):
    size = lax.axis_size("ctx")
    args = list(map(in_hbm, (queries, keys, values, out_grad)))
    swap_x = [(0, 1), (1, 0), (2, 3), (3, 2)]
    swap_y = [(0, 2), (2, 0), (1, 3), (3, 1)]
    xfa, yfa, scale_low, scale_high, fa, fa_steps = load(*args)
    if size == 4:
        got_xa = lax.ppermute(fa, "ctx", swap_x)
    whole = (queries, keys, values, out_grad)
    xfb, yfb, fb, fb_steps = f_states(*whole, scale_high)
    if size == 4:
        got_y1 = lax.ppermute(fb, "ctx", swap_y)
    xga, yga, xgb, ygb, ga_steps, gb_steps, mixed, inner_b = g_states(*whole, scale_low, fb)
    if size == 4:
        got_xb = lax.ppermute(mixed, "ctx", swap_x)
    half_a, half_b = (xfa, yfa, xga, yga), (xfb, yfb, xgb, ygb)
    part_a, part_b = local_terms(half_a), local_terms(half_b)
    if size == 4:
        (sum_a,) = add(fa, got_xa, [(0, HALF)], [part_a[0], part_b[0]])
        got_y2 = lax.ppermute(sum_a, "ctx", swap_y)
        sums = add(got_y1, inner_b, CUTS, [sum_a])
        far_last = [lax.ppermute(s, "ctx", swap_x) for s in sums]
        near_a, near_b = got_xa, got_xb
        far_a, far_b = (got_y2, got_xb), got_y1
        after = sums
    else:
        near_a, near_b = scan_sum(fa, size, 1), scan_sum(fb, size, 1)
        far_a, far_b = (scan_sum(mixed, size, -1),), scan_sum(inner_b, size, -1)
        after = []
    received = (near_a, near_b, *far_a, far_b)
    jobs = [Job((xga, yga, fa_steps, part_a[0], part_a[1], near_a), p, 0, p) for p in range(HALF)]
    jobs += [Job((xgb, ygb, fb_steps, part_b[0], part_b[1], near_b), p, 0, HALF + p) for p in range(HALF)]
    outs = cross_terms(jobs, True, scale_low, [], received, after)
    jobs = [Job((xfa, yfa, ga_steps, part_a[2], part_a[3], *far_a), p, -1, p) for p in range(HALF)]
    outs = cross_terms(jobs, False, scale_high, outs, received)
    for cut, (start, stop) in enumerate(CUTS):
        last = (far_last[cut],) if size == 4 else ()
        arrays = (xfb, yfb, gb_steps, part_b[2], part_b[3], far_b, *last)
        jobs = [Job(arrays, p, p - start, HALF + p) for p in range(start, stop)]
        outs = cross_terms(jobs, False, scale_high, outs, (*received, *last))
    return tuple(outs)


def solution(mesh):
    spec = P(("batch", "ctx"), None)
    return jax.shard_map(local, mesh=mesh, in_specs=(spec,) * 4, out_specs=(spec,) * 4, check_vma=False)
```

```python
import functools
import typing

import jax
import jax.numpy as jnp
from jax import lax
from jax.experimental import pallas as pl
from jax.experimental.pallas import tpu as pltpu
from jax.sharding import PartitionSpec as P


H = 16
DK = 64
DV = 128
PAIRS = H // 2
HALF = PAIRS // 2
XW = 2 * DK
YW = 2 * DV
CHUNK = 128
PIECE = 256
FIRST = HALF
EARLY = 0
LATE = 5
VMEM_LIMIT = 12 * 1024 * 1024

NN = (((1,), (0,)), ((), ()))
NT = (((1,), (1,)), ((), ()))
TN = (((0,), (0,)), ((), ()))
F32 = jnp.float32
BF16 = jnp.bfloat16

HBM = pl.BlockSpec(memory_space=pltpu.HBM)
VMEM = pl.BlockSpec(memory_space=pltpu.VMEM)


def dot(a, b, dims=NN):
    return lax.dot_general(a, b, dims, preferred_element_type=F32)


def is_low():
    size = lax.axis_size("ctx")
    return lax.axis_index("ctx") < (size // 2 if size == 4 else size)


def is_inner():
    at = lax.axis_index("ctx")
    return (at == 1) | (at == 2) if lax.axis_size("ctx") == 4 else at >= 0


def in_vmem(array):
    return pltpu.with_memory_space_constraint(array, pltpu.VMEM)


def in_hbm(array):
    return pltpu.with_memory_space_constraint(array, pltpu.HBM)


def x_shape(length, pairs, dtype=BF16):
    return pltpu.VMEM((length, pairs * XW), dtype)


def y_shape(length, pairs, dtype=BF16):
    return pltpu.VMEM((length, pairs * YW), dtype)


def states_shape(pairs):
    return pltpu.VMEM((pairs, XW, DV), F32)


def steps_shape(length, pairs):
    return pltpu.VMEM((pairs, length // CHUNK, XW, DV), F32)


def params():
    return pltpu.CompilerParams(vmem_limit_bytes=VMEM_LIMIT)


def diagonal(square):
    return jnp.concatenate([square[:DK, :DV], square[DK:, DV:]], axis=0)


def xs(p):
    return slice(p * XW, (p + 1) * XW)


def ys(p):
    return slice(p * YW, (p + 1) * YW)


def chunks_of(array, size=CHUNK):
    return [slice(c, c + size) for c in range(0, array.shape[0], size)]


def twice(scale):
    return jnp.concatenate([scale, scale], axis=1)


class Pair(typing.NamedTuple):
    x: typing.Any
    y: typing.Any
    steps: typing.Any
    at: int


def pairs_of(x, y, steps):
    return [Pair(x, y, steps, i) for i in range(steps.shape[0])]


class Places:
    def __init__(self):
        self.arrays = []

    def __call__(self, array):
        for i, other in enumerate(self.arrays):
            if other is array:
                return i
        self.arrays.append(array)
        return len(self.arrays) - 1


def chunk_states(x, y, first, count, scaled, scale, rows, kept=None):
    states = []
    for p in range(count):
        old, new = x[rows, xs(first + p)], y[rows, ys(first + p)]
        if kept is not None:
            kept[rows, xs(p)] = old
        if scale is not None:
            new = (new.astype(F32) * twice(scale[rows, :])).astype(BF16)
            scaled[rows, ys(p)] = new
        states.append(diagonal(dot(old, new, TN)))
    return states


def block_states(parts, backward, steps):
    count = len(parts)
    states = []
    for p in range(len(parts[0])):
        zero = jnp.zeros_like(parts[0][p])
        before, after = [zero], [zero]
        for c in range(count - 1):
            before.append(before[-1] + parts[c][p])
            after.append(after[-1] + parts[count - 1 - c][p])
        for c in range(count):
            steps[p, c] = jnp.where(backward, after[count - 1 - c], before[c])
        states.append(before[-1] + parts[-1][p])
    return states


def either(low, work, kv, qd):
    @pl.when(low)
    def _():
        work(*kv)

    @pl.when(jnp.logical_not(low))
    def _():
        work(*qd)


def load_kernel(q, k, v, do, x, y, scale_low, scale_high, state, raw, sems):
    low = is_low()
    length = q.shape[0]
    pieces = chunks_of(q, PIECE)

    def copies(a, b):
        return [
            (
                pltpu.make_async_copy(a.at[rows, pl.ds(0, FIRST * XW)], x.at[rows, :], sems.at[0, c]),
                pltpu.make_async_copy(b.at[rows, pl.ds(0, FIRST * YW)], raw.at[rows, :], sems.at[1, c]),
            )
            for c, rows in enumerate(pieces)
        ]

    def start(a, b):
        for pair in copies(a, b):
            for copy in pair:
                copy.start()

    either(low, start, (k, v), (q, do))
    at = lax.axis_index("ctx") * length + lax.broadcasted_iota(jnp.int32, (length, DV), 0)
    scale = 1.0 / jnp.sqrt(DK * (at.astype(F32) + 1.0))
    scale_low[...] = jnp.where(low, scale, 1.0)
    scale_high[...] = jnp.where(low, 1.0, scale)
    total = None
    for rows, pair in zip(pieces, copies(k, v)):
        for copy in pair:
            copy.wait()
        parts = chunk_states(x, raw, 0, FIRST, y, scale_high, rows)
        total = parts if total is None else [a + b for a, b in zip(total, parts)]
    for p, new in enumerate(total):
        state[p] = new


def load(q, k, v, do):
    length = q.shape[0]
    x, y = x_shape(length, FIRST), y_shape(length, FIRST)
    scale = pltpu.VMEM((length, DV), F32)
    return pl.pallas_call(
        load_kernel,
        in_specs=[HBM] * 4,
        out_specs=[VMEM] * 5,
        out_shape=[x, y, scale, scale, states_shape(FIRST)],
        scratch_shapes=[y, pltpu.SemaphoreType.DMA((2, length // PIECE))],
        compiler_params=params(),
        name="load",
    )(*map(in_hbm, (q, k, v, do)))


def f_kernel(q, k, v, do, scale, x, y, steps, state):
    low = is_low()

    def work(a, b):
        parts = [chunk_states(a, b, FIRST, PAIRS - FIRST, y, scale, rows, x) for rows in chunks_of(x)]
        states = block_states(parts, jnp.logical_not(low), steps)
        for p, new in enumerate(states):
            state[p] = new

    either(low, work, (k, v), (q, do))


def f_states(q, k, v, do, scale):
    length, count = q.shape[0], PAIRS - FIRST
    return pl.pallas_call(
        f_kernel,
        in_specs=[VMEM] * 5,
        out_specs=[VMEM] * 4,
        out_shape=[
            x_shape(length, count),
            y_shape(length, count),
            steps_shape(length, count),
            states_shape(count),
        ],
        compiler_params=params(),
        name="f_states",
    )(*map(in_vmem, (q, k, v, do, scale)))


def g_kernel(q, k, v, do, scale, x, y, steps, state):
    low = is_low()

    def work(a, b):
        for first in (0, HALF):
            half_x, half_y = x.at[:, pl.ds(first * XW, HALF * XW)], y.at[:, pl.ds(first * YW, HALF * YW)]
            parts = [chunk_states(a, b, first, HALF, half_y, scale, rows, half_x) for rows in chunks_of(x)]
            for p, new in enumerate(block_states(parts, low, steps.at[pl.ds(first, HALF)])):
                state[first + p] = new

    either(low, work, (q, do), (k, v))


def g_states(q, k, v, do, scale):
    length = q.shape[0]
    return pl.pallas_call(
        g_kernel,
        in_specs=[VMEM] * 5,
        out_specs=[VMEM] * 4,
        out_shape=[x_shape(length, PAIRS), y_shape(length, PAIRS), steps_shape(length, PAIRS), states_shape(PAIRS)],
        compiler_params=params(),
        name="g_states",
    )(*map(in_vmem, (q, k, v, do, scale)))


def steps_kernel(x, y, *refs):
    parts = [chunk_states(x, y, 0, FIRST, None, None, rows) for rows in chunks_of(x)]
    block_states(parts, jnp.logical_not(is_low()), refs[-1])


def first_steps(x, y, after):
    return pl.pallas_call(
        steps_kernel,
        in_specs=[VMEM] * (2 + len(after)),
        out_specs=VMEM,
        out_shape=steps_shape(x.shape[0], FIRST),
        compiler_params=params(),
        name="first_steps",
    )(*map(in_vmem, (x, y, *after)))


def payload_kernel(work, taken, *refs):
    out = refs[-1]
    for p in range(out.shape[0]):
        out[p] = work(p, *refs[:taken])


def payload(name, work, count, ins, after=()):
    return pl.pallas_call(
        functools.partial(payload_kernel, work, len(ins)),
        in_specs=[VMEM] * (len(ins) + len(after)),
        out_specs=VMEM,
        out_shape=states_shape(count),
        compiler_params=params(),
        name=name,
    )(*ins, *map(in_vmem, after))


def head_rows(x):
    lane = lax.broadcasted_iota(jnp.int32, x.shape, 1)
    zero = jnp.zeros_like(x)
    return jnp.concatenate([jnp.where(lane < DK, x, zero), jnp.where(lane >= DK, x, zero)], axis=0)


def head_blocks(y):
    zero = jnp.zeros_like(y[:, :DV])
    top = jnp.concatenate([y[:, :DV], zero], axis=1)
    return jnp.concatenate([top, jnp.concatenate([zero, y[:, DV:]], axis=1)], axis=0)


def state_blocks(state):
    row = lax.broadcasted_iota(jnp.int32, state.shape, 0)
    zero = jnp.zeros_like(state)
    both = jnp.concatenate([jnp.where(row < DK, state, zero), jnp.where(row >= DK, state, zero)], axis=1)
    return both.astype(BF16)


def turned(scores):
    return jnp.concatenate([scores[:, :CHUNK].T, scores[:, CHUNK:].T], axis=1)


def out_copies(staged, at, when_low, when_high, pair, width, sem):
    source = staged.at[:, pl.ds(at * width, width)]
    columns = pl.ds(pair * width, width)
    return [pltpu.make_async_copy(source, target.at[:, columns], sem.at[at]) for target in (when_low, when_high)]


def send(copies, low):
    @pl.when(low)
    def _():
        copies[0].start()

    @pl.when(jnp.logical_not(low))
    def _():
        copies[1].start()


def local_kernel(places, *refs):
    low = is_low()
    o1, o3, o2, o4 = refs[-4:]
    row = lax.broadcasted_iota(jnp.int32, (CHUNK, 2 * CHUNK), 0)
    col = lax.rem(lax.broadcasted_iota(jnp.int32, (CHUNK, 2 * CHUNK), 1), CHUNK)
    keep = jnp.where(low, row - col, col - row) >= 0
    chunks = chunks_of(o1)
    for p, (f, g) in enumerate(places):
        (xf, yf), (xg, yg) = (refs[f.x], refs[f.y]), (refs[g.x], refs[g.y])
        parts, scores = [], []
        for rows in chunks:
            x1, y1, x2, y2 = xf[rows, xs(f.at)], yf[rows, ys(f.at)], xg[rows, xs(g.at)], yg[rows, ys(g.at)]
            parts.append((head_rows(x1), head_blocks(y1), x2, y2))
        for x1s, y1s, x2, y2 in parts:
            m = jnp.where(keep, dot(x2, x1s, NT), 0.0).astype(BF16)
            n = jnp.where(keep, dot(y2, y1s, NT), 0.0).astype(BF16)
            scores.append((m, n))
        for rows, (x1s, y1s, x2, y2), (m, n) in zip(chunks, parts, scores):
            o1[rows, ys(p)] = dot(m, y1s)
            o3[rows, xs(p)] = dot(n, x1s)
            o2[rows, ys(p)] = dot(turned(m), head_blocks(y2))
            o4[rows, xs(p)] = dot(turned(n), head_rows(x2))


def local_terms(f, g, after=()):
    place = Places()
    places = [[Pair(place(s.x), place(s.y), None, s.at) for s in both] for both in zip(f, g)]
    length, count = f[0].x.shape[0], len(f)
    x, y = x_shape(length, count, F32), y_shape(length, count, F32)
    return pl.pallas_call(
        functools.partial(local_kernel, places),
        in_specs=[VMEM] * (len(place.arrays) + len(after)),
        out_specs=[VMEM] * 4,
        out_shape=[y, x, y, x],
        compiler_params=params(),
        name="local",
    )(*map(in_vmem, (*place.arrays, *after)))


ALWAYS, INNER, OUTER = range(3)


class Job(typing.NamedTuple):
    side: Pair
    other: Pair
    wide: typing.Any
    narrow: typing.Any
    at: int
    terms: tuple
    pair: int


def cross_kernel(jobs, near, scale_at, *refs):
    att, qg, kg, vg, wide_out, narrow_out, wide_sem, narrow_sem = refs[-8:]
    low = is_low()
    inner = is_inner()
    scale = refs[scale_at]
    started = []
    for i, job in enumerate(jobs):
        x, y, steps, wide, narrow = [refs[w] for w in (job.side.x, job.side.y, job.other.steps, job.wide, job.narrow)]
        at = job.side.at
        base = None
        for array, where, when in job.terms:
            term = refs[array][where]
            if when != ALWAYS:
                term = jnp.where(inner, term, 0.0) if when == INNER else jnp.where(inner, 0.0, term)
            base = term if base is None else base + term
        chunks = chunks_of(x)
        blocks = [state_blocks(base + steps[job.other.at, c]) for c in range(len(chunks))]
        a = [dot(x[rows, xs(at)], b) for rows, b in zip(chunks, blocks)]
        b = [dot(y[rows, ys(at)], b, NT) for rows, b in zip(chunks, blocks)]
        targets = (att, vg, qg, kg) if near else (vg, att, kg, qg)
        to_wide = out_copies(wide_out, i, targets[0], targets[1], job.pair, YW, wide_sem)
        to_narrow = out_copies(narrow_out, i, targets[2], targets[3], job.pair, XW, narrow_sem)
        for rows, new in zip(chunks, a):
            wide_out[rows, ys(i)] = ((wide[rows, ys(job.at)] + new) * twice(scale[rows, :])).astype(BF16)
        send(to_wide, low)
        for rows, new in zip(chunks, b):
            narrow_out[rows, xs(i)] = (narrow[rows, xs(job.at)] + new).astype(BF16)
        send(to_narrow, low)
        started += [to_wide[0], to_narrow[0]]
    for copy in started:
        copy.wait()


def cross_terms(jobs, near, scale, outs):
    place, received = Places(), Places()
    scale_at = place(scale)
    placed = []
    for job in jobs:
        side = Pair(place(job.side.x), place(job.side.y), None, job.side.at)
        other = Pair(None, None, place(job.other.steps), job.other.at)
        terms = []
        for array, where, when in job.terms:
            received(array)
            terms.append((place(array), where, when))
        placed.append(Job(side, other, place(job.wide), place(job.narrow), job.at, tuple(terms), job.pair))
    length, count = scale.shape[0], len(jobs)
    ins = [a if any(a is r for r in received.arrays) else in_vmem(a) for a in place.arrays]
    wide = jax.ShapeDtypeStruct((length, H * DV), BF16)
    narrow = jax.ShapeDtypeStruct((length, H * DK), BF16)
    return pl.pallas_call(
        functools.partial(cross_kernel, placed, near, scale_at),
        in_specs=[VMEM] * len(ins) + [HBM] * len(outs),
        out_specs=[HBM] * 4,
        out_shape=[wide, narrow, narrow, wide],
        input_output_aliases={len(ins) + i: i for i in range(len(outs))},
        scratch_shapes=[
            pltpu.VMEM((length, count * YW), BF16),
            pltpu.VMEM((length, count * XW), BF16),
            pltpu.SemaphoreType.DMA((count,)),
            pltpu.SemaphoreType.DMA((count,)),
        ],
        compiler_params=params(),
        name="near" if near else "far",
    )(*ins, *outs)


def scan_sum(state, size, sign):
    def moved(array, step):
        return lax.ppermute(array, "ctx", [(i, i + sign * step) for i in range(size) if 0 <= i + sign * step < size])

    total, step = moved(state, 1), 1
    while step < size:
        total, step = total + moved(total, step), 2 * step
    return total


def local(queries, keys, values, out_grad):
    size = lax.axis_size("ctx")
    args = (queries, keys, values, out_grad)
    x1, y1, scale_low, scale_high, fa = load(*args)
    swap_x = functools.partial(lax.ppermute, axis_name="ctx", perm=[(0, 1), (1, 0), (2, 3), (3, 2)])
    swap_y = functools.partial(lax.ppermute, axis_name="ctx", perm=[(0, 2), (2, 0), (1, 3), (3, 1)])
    if size == 4:
        got_xa = swap_x(fa)
    x2, y2, f_steps, fb = f_states(*args, scale_high)
    if size == 4:
        got_y1 = swap_y(fb)
    x, y, g_steps, gs = g_states(*args, scale_low)
    g = pairs_of(x, y, g_steps)
    f = pairs_of(x1, y1, f_steps) + pairs_of(x2, y2, f_steps)
    parts, token = [], []
    if EARLY:
        parts.append(local_terms(f[:EARLY], g[:EARLY]))
        token = parts[0][:1]
    if size == 4:
        mixed = payload("mixed", lambda p, a, b: jnp.where(is_inner(), a[p], b[p]), HALF, (gs, fb), token)
        got_xb = swap_x(mixed)
        parts.append(local_terms(f[EARLY:LATE], g[EARLY:LATE], [mixed]))
        sum_a = payload("swapped", lambda p, a, b: a[p] + b[p], HALF, (fa, got_xa), parts[-1][:1])
        got_y2 = swap_y(sum_a)
        last = payload(
            "summed", lambda p, a, b: a[p] + jnp.where(is_inner(), b[HALF + p], 0.0), HALF, (got_y1, gs), [sum_a]
        )
        got_last = swap_x(last)
        parts.append(local_terms(f[LATE:], g[LATE:], [last]))
        token = [last]
        near = [(array, p, INNER) for array in (got_xa, got_xb) for p in range(HALF)]
        far = [((got_y2, p, ALWAYS), (got_xb, p, OUTER)) for p in range(HALF)]
        far += [((got_y1, p, ALWAYS), (got_last, p, ALWAYS)) for p in range(HALF)]
    else:
        parts += [local_terms(f[EARLY:LATE], g[EARLY:LATE]), local_terms(f[LATE:], g[LATE:])]
        token = []
        near = [(array, p, ALWAYS) for array in [scan_sum(s, size, 1) for s in (fa, fb)] for p in range(HALF)]
        after_me = scan_sum(gs, size, -1)
        far = [((after_me, p, ALWAYS),) for p in range(PAIRS)]
    x1_steps = first_steps(x1, y1, token)
    f[:HALF] = pairs_of(x1, y1, x1_steps)
    local_of = [(part, p) for part in parts for p in range(part[0].shape[1] // YW)]

    def jobs(pairs, side, other, results, terms):
        return [Job(side[p], other[p], local_of[p][0][results], local_of[p][0][results + 1], local_of[p][1], terms(p), p) for p in pairs]

    outs = cross_terms(jobs(range(PAIRS), g, f, 0, lambda p: (near[p],)), True, scale_low, [])
    for pairs in (range(HALF), range(HALF, PAIRS)):
        outs = cross_terms(jobs(pairs, f, g, 2, lambda p: far[p]), False, scale_high, outs)
    return tuple(outs)


def solution(mesh):
    spec = P(("batch", "ctx"), None)
    return jax.shard_map(local, mesh=mesh, in_specs=(spec,) * 4, out_specs=(spec,) * 4, check_vma=False)
```

```python
import functools
import typing

import jax
import jax.numpy as jnp
from jax import lax
from jax.experimental import pallas as pl
from jax.experimental.pallas import tpu as pltpu
from jax.sharding import PartitionSpec as P


H = 16
DK = 64
DV = 128
PAIRS = H // 2
HALF = PAIRS // 2
XW = 2 * DK
YW = 2 * DV
CHUNK = 128
PIECE = 256
FIRST = HALF
EARLY = 0
LATE = 6
CUT = 2
ORDER = range(HALF + CUT), range(HALF + CUT, PAIRS)
VMEM_LIMIT = 12 * 1024 * 1024

NN = (((1,), (0,)), ((), ()))
NT = (((1,), (1,)), ((), ()))
TN = (((0,), (0,)), ((), ()))
F32 = jnp.float32
BF16 = jnp.bfloat16

HBM = pl.BlockSpec(memory_space=pltpu.HBM)
VMEM = pl.BlockSpec(memory_space=pltpu.VMEM)


def dot(a, b, dims=NN):
    return lax.dot_general(a, b, dims, preferred_element_type=F32)


def is_low():
    size = lax.axis_size("ctx")
    return lax.axis_index("ctx") < (size // 2 if size == 4 else size)


def is_inner():
    at = lax.axis_index("ctx")
    return (at == 1) | (at == 2) if lax.axis_size("ctx") == 4 else at >= 0


def in_vmem(array):
    return pltpu.with_memory_space_constraint(array, pltpu.VMEM)


def in_hbm(array):
    return pltpu.with_memory_space_constraint(array, pltpu.HBM)


def x_shape(length, pairs, dtype=BF16):
    return pltpu.VMEM((length, pairs * XW), dtype)


def y_shape(length, pairs, dtype=BF16):
    return pltpu.VMEM((length, pairs * YW), dtype)


def states_shape(pairs):
    return pltpu.VMEM((pairs, XW, DV), F32)


def steps_shape(length, pairs):
    return pltpu.VMEM((pairs, length // CHUNK, XW, DV), F32)


def params():
    return pltpu.CompilerParams(vmem_limit_bytes=VMEM_LIMIT)


def diagonal(square):
    return jnp.concatenate([square[:DK, :DV], square[DK:, DV:]], axis=0)


def xs(p):
    return slice(p * XW, (p + 1) * XW)


def ys(p):
    return slice(p * YW, (p + 1) * YW)


def chunks_of(array, size=CHUNK):
    return [slice(c, c + size) for c in range(0, array.shape[0], size)]


def twice(scale):
    return jnp.concatenate([scale, scale], axis=1)


class Pair(typing.NamedTuple):
    x: typing.Any
    y: typing.Any
    steps: typing.Any
    at: int


def pairs_of(x, y, steps):
    return [Pair(x, y, steps, i) for i in range(steps.shape[0])]


class Places:
    def __init__(self):
        self.arrays = []

    def __call__(self, array):
        for i, other in enumerate(self.arrays):
            if other is array:
                return i
        self.arrays.append(array)
        return len(self.arrays) - 1


def chunk_states(x, y, first, count, scaled, scale, rows, kept=None):
    states = []
    for p in range(count):
        old, new = x[rows, xs(first + p)], y[rows, ys(first + p)]
        if kept is not None:
            kept[rows, xs(p)] = old
        if scale is not None:
            new = (new.astype(F32) * twice(scale[rows, :])).astype(BF16)
            scaled[rows, ys(p)] = new
        states.append(diagonal(dot(old, new, TN)))
    return states


def block_states(parts, backward, steps):
    count = len(parts)
    states = []
    for p in range(len(parts[0])):
        zero = jnp.zeros_like(parts[0][p])
        before, after = [zero], [zero]
        for c in range(count - 1):
            before.append(before[-1] + parts[c][p])
            after.append(after[-1] + parts[count - 1 - c][p])
        for c in range(count):
            steps[p, c] = jnp.where(backward, after[count - 1 - c], before[c])
        states.append(before[-1] + parts[-1][p])
    return states


def either(low, work, kv, qd):
    @pl.when(low)
    def _():
        work(*kv)

    @pl.when(jnp.logical_not(low))
    def _():
        work(*qd)


def load_kernel(q, k, v, do, x, y, scale_low, scale_high, state, raw, sems):
    low = is_low()
    length = q.shape[0]
    pieces = chunks_of(q, PIECE)

    def copies(a, b):
        return [
            (
                pltpu.make_async_copy(a.at[rows, pl.ds(0, FIRST * XW)], x.at[rows, :], sems.at[0, c]),
                pltpu.make_async_copy(b.at[rows, pl.ds(0, FIRST * YW)], raw.at[rows, :], sems.at[1, c]),
            )
            for c, rows in enumerate(pieces)
        ]

    def start(a, b):
        for pair in copies(a, b):
            for copy in pair:
                copy.start()

    either(low, start, (k, v), (q, do))
    at = lax.axis_index("ctx") * length + lax.broadcasted_iota(jnp.int32, (length, DV), 0)
    scale = 1.0 / jnp.sqrt(DK * (at.astype(F32) + 1.0))
    scale_low[...] = jnp.where(low, scale, 1.0)
    scale_high[...] = jnp.where(low, 1.0, scale)
    total = None
    for rows, pair in zip(pieces, copies(k, v)):
        for copy in pair:
            copy.wait()
        parts = chunk_states(x, raw, 0, FIRST, y, scale_high, rows)
        total = parts if total is None else [a + b for a, b in zip(total, parts)]
    for p, new in enumerate(total):
        state[p] = new


def load(q, k, v, do):
    length = q.shape[0]
    x, y = x_shape(length, FIRST), y_shape(length, FIRST)
    scale = pltpu.VMEM((length, DV), F32)
    return pl.pallas_call(
        load_kernel,
        in_specs=[HBM] * 4,
        out_specs=[VMEM] * 5,
        out_shape=[x, y, scale, scale, states_shape(FIRST)],
        scratch_shapes=[y, pltpu.SemaphoreType.DMA((2, length // PIECE))],
        compiler_params=params(),
        name="load",
    )(*map(in_hbm, (q, k, v, do)))


def f_kernel(q, k, v, do, scale, x, y, steps, state):
    low = is_low()

    def work(a, b):
        parts = [chunk_states(a, b, FIRST, PAIRS - FIRST, y, scale, rows, x) for rows in chunks_of(x)]
        states = block_states(parts, jnp.logical_not(low), steps)
        for p, new in enumerate(states):
            state[p] = new

    either(low, work, (k, v), (q, do))


def f_states(q, k, v, do, scale):
    length, count = q.shape[0], PAIRS - FIRST
    return pl.pallas_call(
        f_kernel,
        in_specs=[VMEM] * 5,
        out_specs=[VMEM] * 4,
        out_shape=[
            x_shape(length, count),
            y_shape(length, count),
            steps_shape(length, count),
            states_shape(count),
        ],
        compiler_params=params(),
        name="f_states",
    )(*map(in_vmem, (q, k, v, do, scale)))


def g_kernel(q, k, v, do, scale, x, y, steps, state):
    low = is_low()

    def work(a, b):
        for first in (0, HALF):
            half_x, half_y = x.at[:, pl.ds(first * XW, HALF * XW)], y.at[:, pl.ds(first * YW, HALF * YW)]
            parts = [chunk_states(a, b, first, HALF, half_y, scale, rows, half_x) for rows in chunks_of(x)]
            for p, new in enumerate(block_states(parts, low, steps.at[pl.ds(first, HALF)])):
                state[first + p] = new

    either(low, work, (q, do), (k, v))


def g_states(q, k, v, do, scale):
    length = q.shape[0]
    return pl.pallas_call(
        g_kernel,
        in_specs=[VMEM] * 5,
        out_specs=[VMEM] * 4,
        out_shape=[x_shape(length, PAIRS), y_shape(length, PAIRS), steps_shape(length, PAIRS), states_shape(PAIRS)],
        compiler_params=params(),
        name="g_states",
    )(*map(in_vmem, (q, k, v, do, scale)))


def steps_kernel(x, y, *refs):
    parts = [chunk_states(x, y, 0, FIRST, None, None, rows) for rows in chunks_of(x)]
    block_states(parts, jnp.logical_not(is_low()), refs[-1])


def first_steps(x, y, after):
    return pl.pallas_call(
        steps_kernel,
        in_specs=[VMEM] * (2 + len(after)),
        out_specs=VMEM,
        out_shape=steps_shape(x.shape[0], FIRST),
        compiler_params=params(),
        name="first_steps",
    )(*map(in_vmem, (x, y, *after)))


def payload_kernel(work, taken, *refs):
    out = refs[-1]
    for p in range(out.shape[0]):
        out[p] = work(p, *refs[:taken])


def payload(name, work, count, ins, after=()):
    return pl.pallas_call(
        functools.partial(payload_kernel, work, len(ins)),
        in_specs=[VMEM] * (len(ins) + len(after)),
        out_specs=VMEM,
        out_shape=states_shape(count),
        compiler_params=params(),
        name=name,
    )(*ins, *map(in_vmem, after))


def head_rows(x):
    lane = lax.broadcasted_iota(jnp.int32, x.shape, 1)
    zero = jnp.zeros_like(x)
    return jnp.concatenate([jnp.where(lane < DK, x, zero), jnp.where(lane >= DK, x, zero)], axis=0)


def head_blocks(y):
    zero = jnp.zeros_like(y[:, :DV])
    top = jnp.concatenate([y[:, :DV], zero], axis=1)
    return jnp.concatenate([top, jnp.concatenate([zero, y[:, DV:]], axis=1)], axis=0)


def state_blocks(state):
    row = lax.broadcasted_iota(jnp.int32, state.shape, 0)
    zero = jnp.zeros_like(state)
    both = jnp.concatenate([jnp.where(row < DK, state, zero), jnp.where(row >= DK, state, zero)], axis=1)
    return both.astype(BF16)


def turned(scores):
    return jnp.concatenate([scores[:, :CHUNK].T, scores[:, CHUNK:].T], axis=1)


def out_copies(staged, at, when_low, when_high, pair, width, sem):
    source = staged.at[:, pl.ds(at * width, width)]
    columns = pl.ds(pair * width, width)
    return [pltpu.make_async_copy(source, target.at[:, columns], sem.at[at]) for target in (when_low, when_high)]


def send(copies, low):
    @pl.when(low)
    def _():
        copies[0].start()

    @pl.when(jnp.logical_not(low))
    def _():
        copies[1].start()


def local_kernel(places, *refs):
    low = is_low()
    o1, o3, o2, o4 = refs[-4:]
    row = lax.broadcasted_iota(jnp.int32, (CHUNK, 2 * CHUNK), 0)
    col = lax.rem(lax.broadcasted_iota(jnp.int32, (CHUNK, 2 * CHUNK), 1), CHUNK)
    keep = jnp.where(low, row - col, col - row) >= 0
    chunks = chunks_of(o1)
    for p, (f, g) in enumerate(places):
        (xf, yf), (xg, yg) = (refs[f.x], refs[f.y]), (refs[g.x], refs[g.y])
        parts, scores = [], []
        for rows in chunks:
            x1, y1, x2, y2 = xf[rows, xs(f.at)], yf[rows, ys(f.at)], xg[rows, xs(g.at)], yg[rows, ys(g.at)]
            parts.append((head_rows(x1), head_blocks(y1), x2, y2))
        for x1s, y1s, x2, y2 in parts:
            m = jnp.where(keep, dot(x2, x1s, NT), 0.0).astype(BF16)
            n = jnp.where(keep, dot(y2, y1s, NT), 0.0).astype(BF16)
            scores.append((m, n))
        for rows, (x1s, y1s, x2, y2), (m, n) in zip(chunks, parts, scores):
            o1[rows, ys(p)] = dot(m, y1s)
            o3[rows, xs(p)] = dot(n, x1s)
            o2[rows, ys(p)] = dot(turned(m), head_blocks(y2))
            o4[rows, xs(p)] = dot(turned(n), head_rows(x2))


def local_terms(f, g, after=()):
    place = Places()
    places = [[Pair(place(s.x), place(s.y), None, s.at) for s in both] for both in zip(f, g)]
    length, count = f[0].x.shape[0], len(f)
    x, y = x_shape(length, count, F32), y_shape(length, count, F32)
    return pl.pallas_call(
        functools.partial(local_kernel, places),
        in_specs=[VMEM] * (len(place.arrays) + len(after)),
        out_specs=[VMEM] * 4,
        out_shape=[y, x, y, x],
        compiler_params=params(),
        name="local",
    )(*map(in_vmem, (*place.arrays, *after)))


ALWAYS, INNER, OUTER = range(3)


class Job(typing.NamedTuple):
    side: Pair
    other: Pair
    wide: typing.Any
    narrow: typing.Any
    at: int
    terms: tuple
    pair: int


def cross_kernel(jobs, near, scale_at, *refs):
    att, qg, kg, vg, wide_out, narrow_out, wide_sem, narrow_sem = refs[-8:]
    low = is_low()
    inner = is_inner()
    scale = refs[scale_at]
    started = []
    for i, job in enumerate(jobs):
        x, y, steps, wide, narrow = [refs[w] for w in (job.side.x, job.side.y, job.other.steps, job.wide, job.narrow)]
        at = job.side.at
        base = None
        for array, where, when in job.terms:
            term = refs[array][where]
            if when != ALWAYS:
                term = jnp.where(inner, term, 0.0) if when == INNER else jnp.where(inner, 0.0, term)
            base = term if base is None else base + term
        chunks = chunks_of(x)
        blocks = [state_blocks(base + steps[job.other.at, c]) for c in range(len(chunks))]
        a = [dot(x[rows, xs(at)], b) for rows, b in zip(chunks, blocks)]
        b = [dot(y[rows, ys(at)], b, NT) for rows, b in zip(chunks, blocks)]
        targets = (att, vg, qg, kg) if near else (vg, att, kg, qg)
        to_wide = out_copies(wide_out, i, targets[0], targets[1], job.pair, YW, wide_sem)
        to_narrow = out_copies(narrow_out, i, targets[2], targets[3], job.pair, XW, narrow_sem)
        for rows, new in zip(chunks, a):
            wide_out[rows, ys(i)] = ((wide[rows, ys(job.at)] + new) * twice(scale[rows, :])).astype(BF16)
        send(to_wide, low)
        for rows, new in zip(chunks, b):
            narrow_out[rows, xs(i)] = (narrow[rows, xs(job.at)] + new).astype(BF16)
        send(to_narrow, low)
        started += [to_wide[0], to_narrow[0]]
    for copy in started:
        copy.wait()


def cross_terms(jobs, near, scale, outs, after=()):
    place, received = Places(), Places()
    scale_at = place(scale)
    placed = []
    for job in jobs:
        side = Pair(place(job.side.x), place(job.side.y), None, job.side.at)
        other = Pair(None, None, place(job.other.steps), job.other.at)
        terms = []
        for array, where, when in job.terms:
            received(array)
            terms.append((place(array), where, when))
        placed.append(Job(side, other, place(job.wide), place(job.narrow), job.at, tuple(terms), job.pair))
    length, count = scale.shape[0], len(jobs)
    ins = [a if any(a is r for r in received.arrays) else in_vmem(a) for a in place.arrays]
    wide = jax.ShapeDtypeStruct((length, H * DV), BF16)
    narrow = jax.ShapeDtypeStruct((length, H * DK), BF16)
    return pl.pallas_call(
        functools.partial(cross_kernel, placed, near, scale_at),
        in_specs=[VMEM] * len(ins) + [HBM] * len(outs) + [VMEM] * len(after),
        out_specs=[HBM] * 4,
        out_shape=[wide, narrow, narrow, wide],
        input_output_aliases={len(ins) + i: i for i in range(len(outs))},
        scratch_shapes=[
            pltpu.VMEM((length, count * YW), BF16),
            pltpu.VMEM((length, count * XW), BF16),
            pltpu.SemaphoreType.DMA((count,)),
            pltpu.SemaphoreType.DMA((count,)),
        ],
        compiler_params=params(),
        name="near" if near else "far",
    )(*ins, *outs, *map(in_vmem, after))


def scan_sum(state, size, sign):
    def moved(array, step):
        return lax.ppermute(array, "ctx", [(i, i + sign * step) for i in range(size) if 0 <= i + sign * step < size])

    total, step = moved(state, 1), 1
    while step < size:
        total, step = total + moved(total, step), 2 * step
    return total


def local(queries, keys, values, out_grad):
    size = lax.axis_size("ctx")
    args = (queries, keys, values, out_grad)
    x1, y1, scale_low, scale_high, fa = load(*args)
    swap_x = functools.partial(lax.ppermute, axis_name="ctx", perm=[(0, 1), (1, 0), (2, 3), (3, 2)])
    swap_y = functools.partial(lax.ppermute, axis_name="ctx", perm=[(0, 2), (2, 0), (1, 3), (3, 1)])
    if size == 4:
        got_xa = swap_x(fa)
    x2, y2, f_steps, fb = f_states(*args, scale_high)
    if size == 4:
        got_y1 = swap_y(fb)
    x, y, g_steps, gs = g_states(*args, scale_low)
    g = pairs_of(x, y, g_steps)
    f = pairs_of(x1, y1, f_steps) + pairs_of(x2, y2, f_steps)
    parts, token = [], []
    if EARLY:
        parts.append(local_terms(f[:EARLY], g[:EARLY]))
        token = parts[0][:1]
    if size == 4:
        mixed = payload("mixed", lambda p, a, b: jnp.where(is_inner(), a[p], b[p]), HALF, (gs, fb), token)
        got_xb = swap_x(mixed)
        parts.append(local_terms(f[EARLY:LATE], g[EARLY:LATE], [mixed]))
        sum_a = payload("swapped", lambda p, a, b: a[p] + b[p], HALF, (fa, got_xa), parts[-1][:1])
        got_y2 = swap_y(sum_a)

        def summed(start, stop, after):
            def work(p, got, own):
                return got[start + p] + jnp.where(is_inner(), own[HALF + start + p], 0.0)

            return payload("summed", work, stop - start, (got_y1, gs), after)

        last = [summed(0, CUT, [sum_a])]
        got_last = [swap_x(last[0])]
        parts.append(local_terms(f[LATE:], g[LATE:], last))
        x1_steps = first_steps(x1, y1, last)
        last.append(summed(CUT, HALF, [parts[-1][0], x1_steps]))
        got_last.append(swap_x(last[1]))
        near = [(array, p, INNER) for array in (got_xa, got_xb) for p in range(HALF)]
        far = [((got_y2, p, ALWAYS), (got_xb, p, OUTER)) for p in range(HALF)]
        far += [((got_y1, p, ALWAYS), (got_last[p >= CUT], p % CUT, ALWAYS)) for p in range(HALF)]
        after = last[1:]
    else:
        parts += [local_terms(f[EARLY:LATE], g[EARLY:LATE]), local_terms(f[LATE:], g[LATE:])]
        x1_steps, after = first_steps(x1, y1, []), []
        near = [(array, p, ALWAYS) for array in [scan_sum(s, size, 1) for s in (fa, fb)] for p in range(HALF)]
        after_me = scan_sum(gs, size, -1)
        far = [((after_me, p, ALWAYS),) for p in range(PAIRS)]
    f[:HALF] = pairs_of(x1, y1, x1_steps)
    local_of = [(part, p) for part in parts for p in range(part[0].shape[1] // YW)]

    def jobs(pairs, side, other, results, terms):
        return [Job(side[p], other[p], local_of[p][0][results], local_of[p][0][results + 1], local_of[p][1], terms(p), p) for p in pairs]

    outs = cross_terms(jobs(range(PAIRS), g, f, 0, lambda p: (near[p],)), True, scale_low, [], after)
    for pairs in ORDER:
        outs = cross_terms(jobs(pairs, f, g, 2, lambda p: far[p]), False, scale_high, outs)
    return tuple(outs)


def solution(mesh):
    spec = P(("batch", "ctx"), None)
    return jax.shard_map(local, mesh=mesh, in_specs=(spec,) * 4, out_specs=(spec,) * 4, check_vma=False)
```

```python
import functools
import typing

import jax
import jax.numpy as jnp
from jax import lax
from jax.experimental import pallas as pl
from jax.experimental.pallas import tpu as pltpu
from jax.sharding import PartitionSpec as P


H = 16
DK = 64
DV = 128
PAIRS = H // 2
HALF = PAIRS // 2
XW = 2 * DK
YW = 2 * DV
CHUNK = 128
PARTS = 2
FIRST = HALF
EARLY = 0
LATE = 6
CUT = 2
ORDER = range(HALF + CUT), range(HALF + CUT, PAIRS)
VMEM_LIMIT = 12 * 1024 * 1024

NN = (((1,), (0,)), ((), ()))
NT = (((1,), (1,)), ((), ()))
TN = (((0,), (0,)), ((), ()))
F32 = jnp.float32
BF16 = jnp.bfloat16

HBM = pl.BlockSpec(memory_space=pltpu.HBM)
VMEM = pl.BlockSpec(memory_space=pltpu.VMEM)


def dot(a, b, dims=NN):
    return lax.dot_general(a, b, dims, preferred_element_type=F32)


def is_low():
    size = lax.axis_size("ctx")
    return lax.axis_index("ctx") < (size // 2 if size == 4 else size)


def is_inner():
    at = lax.axis_index("ctx")
    return (at == 1) | (at == 2) if lax.axis_size("ctx") == 4 else at >= 0


def in_vmem(array):
    return pltpu.with_memory_space_constraint(array, pltpu.VMEM)


def in_hbm(array):
    return pltpu.with_memory_space_constraint(array, pltpu.HBM)


def x_shape(length, pairs, dtype=BF16):
    return pltpu.VMEM((length, pairs * XW), dtype)


def y_shape(length, pairs, dtype=BF16):
    return pltpu.VMEM((length, pairs * YW), dtype)


def states_shape(pairs):
    return pltpu.VMEM((pairs, XW, DV), F32)


def steps_shape(length, pairs):
    return pltpu.VMEM((pairs, length // CHUNK, XW, DV), F32)


def params():
    return pltpu.CompilerParams(vmem_limit_bytes=VMEM_LIMIT)


def diagonal(square):
    return jnp.concatenate([square[:DK, :DV], square[DK:, DV:]], axis=0)


def xs(p):
    return slice(p * XW, (p + 1) * XW)


def ys(p):
    return slice(p * YW, (p + 1) * YW)


def chunks_of(array, size=CHUNK):
    return [slice(c, c + size) for c in range(0, array.shape[0], size)]


def twice(scale):
    return jnp.concatenate([scale, scale], axis=1)


class Pair(typing.NamedTuple):
    x: typing.Any
    y: typing.Any
    steps: typing.Any
    at: int


def pairs_of(x, y, steps):
    return [Pair(x, y, steps, i) for i in range(steps.shape[0])]


class Places:
    def __init__(self):
        self.arrays = []

    def __call__(self, array):
        for i, other in enumerate(self.arrays):
            if other is array:
                return i
        self.arrays.append(array)
        return len(self.arrays) - 1


def chunk_states(x, y, first, count, scaled, scale, rows, kept=None):
    states = []
    for p in range(count):
        old, new = x[rows, xs(first + p)], y[rows, ys(first + p)]
        if kept is not None:
            kept[rows, xs(p)] = old
        if scale is not None:
            new = (new.astype(F32) * twice(scale[rows, :])).astype(BF16)
            scaled[rows, ys(p)] = new
        states.append(diagonal(dot(old, new, TN)))
    return states


def block_states(parts, backward, steps):
    count = len(parts)
    states = []
    for p in range(len(parts[0])):
        zero = jnp.zeros_like(parts[0][p])
        before, after = [zero], [zero]
        for c in range(count - 1):
            before.append(before[-1] + parts[c][p])
            after.append(after[-1] + parts[count - 1 - c][p])
        for c in range(count):
            steps[p, c] = jnp.where(backward, after[count - 1 - c], before[c])
        states.append(before[-1] + parts[-1][p])
    return states


def either(low, work, kv, qd):
    @pl.when(low)
    def _():
        work(*kv)

    @pl.when(jnp.logical_not(low))
    def _():
        work(*qd)


def load_kernel(q, k, v, do, x, y, scale_low, scale_high, state, raw, sems):
    low = is_low()
    length = q.shape[0]
    count = FIRST // PARTS

    def copies(a, b):
        return [
            (
                pltpu.make_async_copy(a.at[:, narrow], x.at[:, narrow], sems.at[0, c]),
                pltpu.make_async_copy(b.at[:, wide], raw.at[:, wide], sems.at[1, c]),
            )
            for c in range(PARTS)
            for narrow, wide in [(pl.ds(c * count * XW, count * XW), pl.ds(c * count * YW, count * YW))]
        ]

    def start(a, b):
        for pair in copies(a, b):
            for copy in pair:
                copy.start()

    either(low, start, (k, v), (q, do))
    at = lax.axis_index("ctx") * length + lax.broadcasted_iota(jnp.int32, (length, DV), 0)
    scale = 1.0 / jnp.sqrt(DK * (at.astype(F32) + 1.0))
    scale_low[...] = jnp.where(low, scale, 1.0)
    scale_high[...] = jnp.where(low, 1.0, scale)
    for c, pair in enumerate(copies(k, v)):
        for copy in pair:
            copy.wait()
        target = y.at[:, pl.ds(c * count * YW, count * YW)]
        for p, new in enumerate(chunk_states(x, raw, c * count, count, target, scale_high, slice(0, length))):
            state[c * count + p] = new


def load(q, k, v, do):
    length = q.shape[0]
    x, y = x_shape(length, FIRST), y_shape(length, FIRST)
    scale = pltpu.VMEM((length, DV), F32)
    return pl.pallas_call(
        load_kernel,
        in_specs=[HBM] * 4,
        out_specs=[VMEM] * 5,
        out_shape=[x, y, scale, scale, states_shape(FIRST)],
        scratch_shapes=[y, pltpu.SemaphoreType.DMA((2, PARTS))],
        compiler_params=params(),
        name="load",
    )(*map(in_hbm, (q, k, v, do)))


def f_kernel(q, k, v, do, scale, x, y, steps, state):
    low = is_low()

    def work(a, b):
        parts = [chunk_states(a, b, FIRST, PAIRS - FIRST, y, scale, rows, x) for rows in chunks_of(x)]
        states = block_states(parts, jnp.logical_not(low), steps)
        for p, new in enumerate(states):
            state[p] = new

    either(low, work, (k, v), (q, do))


def f_states(q, k, v, do, scale):
    length, count = q.shape[0], PAIRS - FIRST
    return pl.pallas_call(
        f_kernel,
        in_specs=[VMEM] * 5,
        out_specs=[VMEM] * 4,
        out_shape=[
            x_shape(length, count),
            y_shape(length, count),
            steps_shape(length, count),
            states_shape(count),
        ],
        compiler_params=params(),
        name="f_states",
    )(*map(in_vmem, (q, k, v, do, scale)))


def g_kernel(q, k, v, do, scale, x, y, steps, state):
    low = is_low()

    def work(a, b):
        for first in (0, HALF):
            half_x, half_y = x.at[:, pl.ds(first * XW, HALF * XW)], y.at[:, pl.ds(first * YW, HALF * YW)]
            parts = [chunk_states(a, b, first, HALF, half_y, scale, rows, half_x) for rows in chunks_of(x)]
            for p, new in enumerate(block_states(parts, low, steps.at[pl.ds(first, HALF)])):
                state[first + p] = new

    either(low, work, (q, do), (k, v))


def g_states(q, k, v, do, scale):
    length = q.shape[0]
    return pl.pallas_call(
        g_kernel,
        in_specs=[VMEM] * 5,
        out_specs=[VMEM] * 4,
        out_shape=[x_shape(length, PAIRS), y_shape(length, PAIRS), steps_shape(length, PAIRS), states_shape(PAIRS)],
        compiler_params=params(),
        name="g_states",
    )(*map(in_vmem, (q, k, v, do, scale)))


def steps_kernel(x, y, *refs):
    parts = [chunk_states(x, y, 0, FIRST, None, None, rows) for rows in chunks_of(x)]
    block_states(parts, jnp.logical_not(is_low()), refs[-1])


def first_steps(x, y, after):
    return pl.pallas_call(
        steps_kernel,
        in_specs=[VMEM] * (2 + len(after)),
        out_specs=VMEM,
        out_shape=steps_shape(x.shape[0], FIRST),
        compiler_params=params(),
        name="first_steps",
    )(*map(in_vmem, (x, y, *after)))


def payload_kernel(work, taken, *refs):
    out = refs[-1]
    for p in range(out.shape[0]):
        out[p] = work(p, *refs[:taken])


def payload(name, work, count, ins, after=()):
    return pl.pallas_call(
        functools.partial(payload_kernel, work, len(ins)),
        in_specs=[VMEM] * (len(ins) + len(after)),
        out_specs=VMEM,
        out_shape=states_shape(count),
        compiler_params=params(),
        name=name,
    )(*ins, *map(in_vmem, after))


def head_rows(x):
    lane = lax.broadcasted_iota(jnp.int32, x.shape, 1)
    zero = jnp.zeros_like(x)
    return jnp.concatenate([jnp.where(lane < DK, x, zero), jnp.where(lane >= DK, x, zero)], axis=0)


def head_blocks(y):
    zero = jnp.zeros_like(y[:, :DV])
    top = jnp.concatenate([y[:, :DV], zero], axis=1)
    return jnp.concatenate([top, jnp.concatenate([zero, y[:, DV:]], axis=1)], axis=0)


def state_blocks(state):
    row = lax.broadcasted_iota(jnp.int32, state.shape, 0)
    zero = jnp.zeros_like(state)
    both = jnp.concatenate([jnp.where(row < DK, state, zero), jnp.where(row >= DK, state, zero)], axis=1)
    return both.astype(BF16)


def turned(scores):
    return jnp.concatenate([scores[:, :CHUNK].T, scores[:, CHUNK:].T], axis=1)


def out_copies(staged, at, when_low, when_high, pair, width, sem):
    source = staged.at[:, pl.ds(at * width, width)]
    columns = pl.ds(pair * width, width)
    return [pltpu.make_async_copy(source, target.at[:, columns], sem.at[at]) for target in (when_low, when_high)]


def send(copies, low):
    @pl.when(low)
    def _():
        copies[0].start()

    @pl.when(jnp.logical_not(low))
    def _():
        copies[1].start()


def local_kernel(places, *refs):
    low = is_low()
    o1, o3, o2, o4 = refs[-4:]
    row = lax.broadcasted_iota(jnp.int32, (CHUNK, 2 * CHUNK), 0)
    col = lax.rem(lax.broadcasted_iota(jnp.int32, (CHUNK, 2 * CHUNK), 1), CHUNK)
    keep = jnp.where(low, row - col, col - row) >= 0
    chunks = chunks_of(o1)
    for p, (f, g) in enumerate(places):
        (xf, yf), (xg, yg) = (refs[f.x], refs[f.y]), (refs[g.x], refs[g.y])
        parts, scores = [], []
        for rows in chunks:
            x1, y1, x2, y2 = xf[rows, xs(f.at)], yf[rows, ys(f.at)], xg[rows, xs(g.at)], yg[rows, ys(g.at)]
            parts.append((head_rows(x1), head_blocks(y1), x2, y2))
        for x1s, y1s, x2, y2 in parts:
            m = jnp.where(keep, dot(x2, x1s, NT), 0.0).astype(BF16)
            n = jnp.where(keep, dot(y2, y1s, NT), 0.0).astype(BF16)
            scores.append((m, n))
        for rows, (x1s, y1s, x2, y2), (m, n) in zip(chunks, parts, scores):
            o1[rows, ys(p)] = dot(m, y1s)
            o3[rows, xs(p)] = dot(n, x1s)
            o2[rows, ys(p)] = dot(turned(m), head_blocks(y2))
            o4[rows, xs(p)] = dot(turned(n), head_rows(x2))


def local_terms(f, g, after=()):
    place = Places()
    places = [[Pair(place(s.x), place(s.y), None, s.at) for s in both] for both in zip(f, g)]
    length, count = f[0].x.shape[0], len(f)
    x, y = x_shape(length, count, F32), y_shape(length, count, F32)
    return pl.pallas_call(
        functools.partial(local_kernel, places),
        in_specs=[VMEM] * (len(place.arrays) + len(after)),
        out_specs=[VMEM] * 4,
        out_shape=[y, x, y, x],
        compiler_params=params(),
        name="local",
    )(*map(in_vmem, (*place.arrays, *after)))


ALWAYS, INNER, OUTER = range(3)


class Job(typing.NamedTuple):
    side: Pair
    other: Pair
    wide: typing.Any
    narrow: typing.Any
    at: int
    terms: tuple
    pair: int


def cross_kernel(jobs, near, scale_at, *refs):
    att, qg, kg, vg, wide_out, narrow_out, wide_sem, narrow_sem = refs[-8:]
    low = is_low()
    inner = is_inner()
    scale = refs[scale_at]
    started = []
    for i, job in enumerate(jobs):
        x, y, steps, wide, narrow = [refs[w] for w in (job.side.x, job.side.y, job.other.steps, job.wide, job.narrow)]
        at = job.side.at
        base = None
        for array, where, when in job.terms:
            term = refs[array][where]
            if when != ALWAYS:
                term = jnp.where(inner, term, 0.0) if when == INNER else jnp.where(inner, 0.0, term)
            base = term if base is None else base + term
        chunks = chunks_of(x)
        blocks = [state_blocks(base + steps[job.other.at, c]) for c in range(len(chunks))]
        a = [dot(x[rows, xs(at)], b) for rows, b in zip(chunks, blocks)]
        b = [dot(y[rows, ys(at)], b, NT) for rows, b in zip(chunks, blocks)]
        targets = (att, vg, qg, kg) if near else (vg, att, kg, qg)
        to_wide = out_copies(wide_out, i, targets[0], targets[1], job.pair, YW, wide_sem)
        to_narrow = out_copies(narrow_out, i, targets[2], targets[3], job.pair, XW, narrow_sem)
        for rows, new in zip(chunks, a):
            wide_out[rows, ys(i)] = ((wide[rows, ys(job.at)] + new) * twice(scale[rows, :])).astype(BF16)
        send(to_wide, low)
        for rows, new in zip(chunks, b):
            narrow_out[rows, xs(i)] = (narrow[rows, xs(job.at)] + new).astype(BF16)
        send(to_narrow, low)
        started += [to_wide[0], to_narrow[0]]
    for copy in started:
        copy.wait()


def cross_terms(jobs, near, scale, outs, after=()):
    place, received = Places(), Places()
    scale_at = place(scale)
    placed = []
    for job in jobs:
        side = Pair(place(job.side.x), place(job.side.y), None, job.side.at)
        other = Pair(None, None, place(job.other.steps), job.other.at)
        terms = []
        for array, where, when in job.terms:
            received(array)
            terms.append((place(array), where, when))
        placed.append(Job(side, other, place(job.wide), place(job.narrow), job.at, tuple(terms), job.pair))
    length, count = scale.shape[0], len(jobs)
    ins = [a if any(a is r for r in received.arrays) else in_vmem(a) for a in place.arrays]
    wide = jax.ShapeDtypeStruct((length, H * DV), BF16)
    narrow = jax.ShapeDtypeStruct((length, H * DK), BF16)
    return pl.pallas_call(
        functools.partial(cross_kernel, placed, near, scale_at),
        in_specs=[VMEM] * len(ins) + [HBM] * len(outs) + [VMEM] * len(after),
        out_specs=[HBM] * 4,
        out_shape=[wide, narrow, narrow, wide],
        input_output_aliases={len(ins) + i: i for i in range(len(outs))},
        scratch_shapes=[
            pltpu.VMEM((length, count * YW), BF16),
            pltpu.VMEM((length, count * XW), BF16),
            pltpu.SemaphoreType.DMA((count,)),
            pltpu.SemaphoreType.DMA((count,)),
        ],
        compiler_params=params(),
        name="near" if near else "far",
    )(*ins, *outs, *map(in_vmem, after))


def scan_sum(state, size, sign):
    def moved(array, step):
        return lax.ppermute(array, "ctx", [(i, i + sign * step) for i in range(size) if 0 <= i + sign * step < size])

    total, step = moved(state, 1), 1
    while step < size:
        total, step = total + moved(total, step), 2 * step
    return total


def local(queries, keys, values, out_grad):
    size = lax.axis_size("ctx")
    args = (queries, keys, values, out_grad)
    x1, y1, scale_low, scale_high, fa = load(*args)
    swap_x = functools.partial(lax.ppermute, axis_name="ctx", perm=[(0, 1), (1, 0), (2, 3), (3, 2)])
    swap_y = functools.partial(lax.ppermute, axis_name="ctx", perm=[(0, 2), (2, 0), (1, 3), (3, 1)])
    if size == 4:
        got_xa = swap_x(fa)
    x2, y2, f_steps, fb = f_states(*args, scale_high)
    if size == 4:
        got_y1 = swap_y(fb)
    x, y, g_steps, gs = g_states(*args, scale_low)
    g = pairs_of(x, y, g_steps)
    f = pairs_of(x1, y1, f_steps) + pairs_of(x2, y2, f_steps)
    parts, token = [], []
    if EARLY:
        parts.append(local_terms(f[:EARLY], g[:EARLY]))
        token = parts[0][:1]
    if size == 4:
        mixed = payload("mixed", lambda p, a, b: jnp.where(is_inner(), a[p], b[p]), HALF, (gs, fb), token)
        got_xb = swap_x(mixed)
        parts.append(local_terms(f[EARLY:LATE], g[EARLY:LATE], [mixed]))
        sum_a = payload("swapped", lambda p, a, b: a[p] + b[p], HALF, (fa, got_xa), parts[-1][:1])
        got_y2 = swap_y(sum_a)

        def summed(start, stop, after):
            def work(p, got, own):
                return got[start + p] + jnp.where(is_inner(), own[HALF + start + p], 0.0)

            return payload("summed", work, stop - start, (got_y1, gs), after)

        last = [summed(0, CUT, [sum_a])]
        got_last = [swap_x(last[0])]
        parts.append(local_terms(f[LATE:], g[LATE:], last))
        x1_steps = first_steps(x1, y1, last)
        last.append(summed(CUT, HALF, [parts[-1][0], x1_steps]))
        got_last.append(swap_x(last[1]))
        near = [(array, p, INNER) for array in (got_xa, got_xb) for p in range(HALF)]
        far = [((got_y2, p, ALWAYS), (got_xb, p, OUTER)) for p in range(HALF)]
        far += [((got_y1, p, ALWAYS), (got_last[p >= CUT], p % CUT, ALWAYS)) for p in range(HALF)]
        after = last[1:]
    else:
        parts += [local_terms(f[EARLY:LATE], g[EARLY:LATE]), local_terms(f[LATE:], g[LATE:])]
        x1_steps, after = first_steps(x1, y1, []), []
        near = [(array, p, ALWAYS) for array in [scan_sum(s, size, 1) for s in (fa, fb)] for p in range(HALF)]
        after_me = scan_sum(gs, size, -1)
        far = [((after_me, p, ALWAYS),) for p in range(PAIRS)]
    f[:HALF] = pairs_of(x1, y1, x1_steps)
    local_of = [(part, p) for part in parts for p in range(part[0].shape[1] // YW)]

    def jobs(pairs, side, other, results, terms):
        return [Job(side[p], other[p], local_of[p][0][results], local_of[p][0][results + 1], local_of[p][1], terms(p), p) for p in pairs]

    outs = cross_terms(jobs(range(PAIRS), g, f, 0, lambda p: (near[p],)), True, scale_low, [], after)
    for pairs in ORDER:
        outs = cross_terms(jobs(pairs, f, g, 2, lambda p: far[p]), False, scale_high, outs)
    return tuple(outs)


def solution(mesh):
    spec = P(("batch", "ctx"), None)
    return jax.shard_map(local, mesh=mesh, in_specs=(spec,) * 4, out_specs=(spec,) * 4, check_vma=False)
```

```python
import functools
import typing

import jax
import jax.numpy as jnp
from jax import lax
from jax.experimental import pallas as pl
from jax.experimental.pallas import tpu as pltpu
from jax.sharding import PartitionSpec as P


H = 16
DK = 64
DV = 128
PAIRS = H // 2
HALF = PAIRS // 2
XW = 2 * DK
YW = 2 * DV
CHUNK = 128
PIECE = 256
FIRST = HALF
EARLY = 0
LATE = 7
CUT = 2
ORDER = range(HALF + CUT), range(HALF + CUT, PAIRS)
VMEM_LIMIT = 12 * 1024 * 1024

NN = (((1,), (0,)), ((), ()))
NT = (((1,), (1,)), ((), ()))
TN = (((0,), (0,)), ((), ()))
F32 = jnp.float32
BF16 = jnp.bfloat16

HBM = pl.BlockSpec(memory_space=pltpu.HBM)
VMEM = pl.BlockSpec(memory_space=pltpu.VMEM)


def dot(a, b, dims=NN):
    return lax.dot_general(a, b, dims, preferred_element_type=F32)


def is_low():
    size = lax.axis_size("ctx")
    return lax.axis_index("ctx") < (size // 2 if size == 4 else size)


def is_inner():
    at = lax.axis_index("ctx")
    return (at == 1) | (at == 2) if lax.axis_size("ctx") == 4 else at >= 0


def in_vmem(array):
    return pltpu.with_memory_space_constraint(array, pltpu.VMEM)


def in_hbm(array):
    return pltpu.with_memory_space_constraint(array, pltpu.HBM)


def x_shape(length, pairs, dtype=BF16):
    return pltpu.VMEM((length, pairs * XW), dtype)


def y_shape(length, pairs, dtype=BF16):
    return pltpu.VMEM((length, pairs * YW), dtype)


def states_shape(pairs):
    return pltpu.VMEM((pairs, XW, DV), F32)


def steps_shape(length, pairs):
    return pltpu.VMEM((pairs, length // CHUNK, XW, DV), F32)


def params():
    return pltpu.CompilerParams(vmem_limit_bytes=VMEM_LIMIT)


def diagonal(square):
    return jnp.concatenate([square[:DK, :DV], square[DK:, DV:]], axis=0)


def xs(p):
    return slice(p * XW, (p + 1) * XW)


def ys(p):
    return slice(p * YW, (p + 1) * YW)


def chunks_of(array, size=CHUNK):
    return [slice(c, c + size) for c in range(0, array.shape[0], size)]


def twice(scale):
    return jnp.concatenate([scale, scale], axis=1)


class Pair(typing.NamedTuple):
    x: typing.Any
    y: typing.Any
    steps: typing.Any
    at: int


def pairs_of(x, y, steps):
    return [Pair(x, y, steps, i) for i in range(steps.shape[0])]


class Places:
    def __init__(self):
        self.arrays = []

    def __call__(self, array):
        for i, other in enumerate(self.arrays):
            if other is array:
                return i
        self.arrays.append(array)
        return len(self.arrays) - 1


def chunk_states(x, y, first, count, scaled, scale, rows, kept=None):
    states = []
    for p in range(count):
        old, new = x[rows, xs(first + p)], y[rows, ys(first + p)]
        if kept is not None:
            kept[rows, xs(p)] = old
        if scale is not None:
            new = (new.astype(F32) * twice(scale[rows, :])).astype(BF16)
            scaled[rows, ys(p)] = new
        states.append(diagonal(dot(old, new, TN)))
    return states


def block_states(parts, backward, steps):
    count = len(parts)
    states = []
    for p in range(len(parts[0])):
        zero = jnp.zeros_like(parts[0][p])
        before, after = [zero], [zero]
        for c in range(count - 1):
            before.append(before[-1] + parts[c][p])
            after.append(after[-1] + parts[count - 1 - c][p])
        for c in range(count):
            steps[p, c] = jnp.where(backward, after[count - 1 - c], before[c])
        states.append(before[-1] + parts[-1][p])
    return states


def either(low, work, kv, qd):
    @pl.when(low)
    def _():
        work(*kv)

    @pl.when(jnp.logical_not(low))
    def _():
        work(*qd)


def load_kernel(q, k, v, do, x, y, scale_low, scale_high, state, raw, sems):
    low = is_low()
    length = q.shape[0]
    pieces = chunks_of(q, PIECE)

    def copies(a, b):
        return [
            (
                pltpu.make_async_copy(a.at[rows, pl.ds(0, FIRST * XW)], x.at[rows, :], sems.at[0, c]),
                pltpu.make_async_copy(b.at[rows, pl.ds(0, FIRST * YW)], raw.at[rows, :], sems.at[1, c]),
            )
            for c, rows in enumerate(pieces)
        ]

    def start(a, b):
        for pair in copies(a, b):
            for copy in pair:
                copy.start()

    either(low, start, (k, v), (q, do))
    at = lax.axis_index("ctx") * length + lax.broadcasted_iota(jnp.int32, (length, DV), 0)
    scale = 1.0 / jnp.sqrt(DK * (at.astype(F32) + 1.0))
    scale_low[...] = jnp.where(low, scale, 1.0)
    scale_high[...] = jnp.where(low, 1.0, scale)
    total = None
    for rows, pair in zip(pieces, copies(k, v)):
        for copy in pair:
            copy.wait()
        parts = chunk_states(x, raw, 0, FIRST, y, scale_high, rows)
        total = parts if total is None else [a + b for a, b in zip(total, parts)]
    for p, new in enumerate(total):
        state[p] = new


def load(q, k, v, do):
    length = q.shape[0]
    x, y = x_shape(length, FIRST), y_shape(length, FIRST)
    scale = pltpu.VMEM((length, DV), F32)
    return pl.pallas_call(
        load_kernel,
        in_specs=[HBM] * 4,
        out_specs=[VMEM] * 5,
        out_shape=[x, y, scale, scale, states_shape(FIRST)],
        scratch_shapes=[y, pltpu.SemaphoreType.DMA((2, length // PIECE))],
        compiler_params=params(),
        name="load",
    )(*map(in_hbm, (q, k, v, do)))


def f_kernel(q, k, v, do, scale, x, y, steps, state):
    low = is_low()

    def work(a, b):
        parts = [chunk_states(a, b, FIRST, PAIRS - FIRST, y, scale, rows, x) for rows in chunks_of(x)]
        states = block_states(parts, jnp.logical_not(low), steps)
        for p, new in enumerate(states):
            state[p] = new

    either(low, work, (k, v), (q, do))


def f_states(q, k, v, do, scale):
    length, count = q.shape[0], PAIRS - FIRST
    return pl.pallas_call(
        f_kernel,
        in_specs=[VMEM] * 5,
        out_specs=[VMEM] * 4,
        out_shape=[
            x_shape(length, count),
            y_shape(length, count),
            steps_shape(length, count),
            states_shape(count),
        ],
        compiler_params=params(),
        name="f_states",
    )(*map(in_vmem, (q, k, v, do, scale)))


def g_kernel(q, k, v, do, scale, x, y, steps, state):
    low = is_low()

    def work(a, b):
        for first in (0, HALF):
            half_x, half_y = x.at[:, pl.ds(first * XW, HALF * XW)], y.at[:, pl.ds(first * YW, HALF * YW)]
            parts = [chunk_states(a, b, first, HALF, half_y, scale, rows, half_x) for rows in chunks_of(x)]
            for p, new in enumerate(block_states(parts, low, steps.at[pl.ds(first, HALF)])):
                state[first + p] = new

    either(low, work, (q, do), (k, v))


def g_states(q, k, v, do, scale):
    length = q.shape[0]
    return pl.pallas_call(
        g_kernel,
        in_specs=[VMEM] * 5,
        out_specs=[VMEM] * 4,
        out_shape=[x_shape(length, PAIRS), y_shape(length, PAIRS), steps_shape(length, PAIRS), states_shape(PAIRS)],
        compiler_params=params(),
        name="g_states",
    )(*map(in_vmem, (q, k, v, do, scale)))


def steps_kernel(x, y, *refs):
    parts = [chunk_states(x, y, 0, FIRST, None, None, rows) for rows in chunks_of(x)]
    block_states(parts, jnp.logical_not(is_low()), refs[-1])


def first_steps(x, y, after):
    return pl.pallas_call(
        steps_kernel,
        in_specs=[VMEM] * (2 + len(after)),
        out_specs=VMEM,
        out_shape=steps_shape(x.shape[0], FIRST),
        compiler_params=params(),
        name="first_steps",
    )(*map(in_vmem, (x, y, *after)))


def payload_kernel(work, taken, *refs):
    out = refs[-1]
    for p in range(out.shape[0]):
        out[p] = work(p, *refs[:taken])


def payload(name, work, count, ins, after=()):
    return pl.pallas_call(
        functools.partial(payload_kernel, work, len(ins)),
        in_specs=[VMEM] * (len(ins) + len(after)),
        out_specs=VMEM,
        out_shape=states_shape(count),
        compiler_params=params(),
        name=name,
    )(*ins, *map(in_vmem, after))


def head_rows(x):
    lane = lax.broadcasted_iota(jnp.int32, x.shape, 1)
    zero = jnp.zeros_like(x)
    return jnp.concatenate([jnp.where(lane < DK, x, zero), jnp.where(lane >= DK, x, zero)], axis=0)


def head_blocks(y):
    zero = jnp.zeros_like(y[:, :DV])
    top = jnp.concatenate([y[:, :DV], zero], axis=1)
    return jnp.concatenate([top, jnp.concatenate([zero, y[:, DV:]], axis=1)], axis=0)


def state_blocks(state):
    row = lax.broadcasted_iota(jnp.int32, state.shape, 0)
    zero = jnp.zeros_like(state)
    both = jnp.concatenate([jnp.where(row < DK, state, zero), jnp.where(row >= DK, state, zero)], axis=1)
    return both.astype(BF16)


def turned(scores):
    return jnp.concatenate([scores[:, :CHUNK].T, scores[:, CHUNK:].T], axis=1)


def out_copies(staged, at, when_low, when_high, pair, width, sem):
    source = staged.at[:, pl.ds(at * width, width)]
    columns = pl.ds(pair * width, width)
    return [pltpu.make_async_copy(source, target.at[:, columns], sem.at[at]) for target in (when_low, when_high)]


def send(copies, low):
    @pl.when(low)
    def _():
        copies[0].start()

    @pl.when(jnp.logical_not(low))
    def _():
        copies[1].start()


def local_kernel(places, *refs):
    low = is_low()
    o1, o3, o2, o4 = refs[-4:]
    row = lax.broadcasted_iota(jnp.int32, (CHUNK, 2 * CHUNK), 0)
    col = lax.rem(lax.broadcasted_iota(jnp.int32, (CHUNK, 2 * CHUNK), 1), CHUNK)
    keep = jnp.where(low, row - col, col - row) >= 0
    chunks = chunks_of(o1)
    for p, (f, g) in enumerate(places):
        (xf, yf), (xg, yg) = (refs[f.x], refs[f.y]), (refs[g.x], refs[g.y])
        parts, scores = [], []
        for rows in chunks:
            x1, y1, x2, y2 = xf[rows, xs(f.at)], yf[rows, ys(f.at)], xg[rows, xs(g.at)], yg[rows, ys(g.at)]
            parts.append((head_rows(x1), head_blocks(y1), x2, y2))
        for x1s, y1s, x2, y2 in parts:
            m = jnp.where(keep, dot(x2, x1s, NT), 0.0).astype(BF16)
            n = jnp.where(keep, dot(y2, y1s, NT), 0.0).astype(BF16)
            scores.append((m, n))
        for rows, (x1s, y1s, x2, y2), (m, n) in zip(chunks, parts, scores):
            o1[rows, ys(p)] = dot(m, y1s)
            o3[rows, xs(p)] = dot(n, x1s)
            o2[rows, ys(p)] = dot(turned(m), head_blocks(y2))
            o4[rows, xs(p)] = dot(turned(n), head_rows(x2))


def local_terms(f, g, after=()):
    place = Places()
    places = [[Pair(place(s.x), place(s.y), None, s.at) for s in both] for both in zip(f, g)]
    length, count = f[0].x.shape[0], len(f)
    x, y = x_shape(length, count, F32), y_shape(length, count, F32)
    return pl.pallas_call(
        functools.partial(local_kernel, places),
        in_specs=[VMEM] * (len(place.arrays) + len(after)),
        out_specs=[VMEM] * 4,
        out_shape=[y, x, y, x],
        compiler_params=params(),
        name="local",
    )(*map(in_vmem, (*place.arrays, *after)))


ALWAYS, INNER, OUTER = range(3)


class Job(typing.NamedTuple):
    side: Pair
    other: Pair
    wide: typing.Any
    narrow: typing.Any
    at: int
    terms: tuple
    pair: int


def cross_kernel(jobs, near, scale_at, *refs):
    att, qg, kg, vg, wide_out, narrow_out, wide_sem, narrow_sem = refs[-8:]
    low = is_low()
    inner = is_inner()
    scale = refs[scale_at]
    started = []
    for i, job in enumerate(jobs):
        x, y, steps, wide, narrow = [refs[w] for w in (job.side.x, job.side.y, job.other.steps, job.wide, job.narrow)]
        at = job.side.at
        base = None
        for array, where, when in job.terms:
            term = refs[array][where]
            if when != ALWAYS:
                term = jnp.where(inner, term, 0.0) if when == INNER else jnp.where(inner, 0.0, term)
            base = term if base is None else base + term
        chunks = chunks_of(x)
        blocks = [state_blocks(base + steps[job.other.at, c]) for c in range(len(chunks))]
        a = [dot(x[rows, xs(at)], b) for rows, b in zip(chunks, blocks)]
        b = [dot(y[rows, ys(at)], b, NT) for rows, b in zip(chunks, blocks)]
        targets = (att, vg, qg, kg) if near else (vg, att, kg, qg)
        to_wide = out_copies(wide_out, i, targets[0], targets[1], job.pair, YW, wide_sem)
        to_narrow = out_copies(narrow_out, i, targets[2], targets[3], job.pair, XW, narrow_sem)
        for rows, new in zip(chunks, a):
            wide_out[rows, ys(i)] = ((wide[rows, ys(job.at)] + new) * twice(scale[rows, :])).astype(BF16)
        send(to_wide, low)
        for rows, new in zip(chunks, b):
            narrow_out[rows, xs(i)] = (narrow[rows, xs(job.at)] + new).astype(BF16)
        send(to_narrow, low)
        started += [to_wide[0], to_narrow[0]]
    for copy in started:
        copy.wait()


def cross_terms(jobs, near, scale, outs, after=()):
    place, received = Places(), Places()
    scale_at = place(scale)
    placed = []
    for job in jobs:
        side = Pair(place(job.side.x), place(job.side.y), None, job.side.at)
        other = Pair(None, None, place(job.other.steps), job.other.at)
        terms = []
        for array, where, when in job.terms:
            received(array)
            terms.append((place(array), where, when))
        placed.append(Job(side, other, place(job.wide), place(job.narrow), job.at, tuple(terms), job.pair))
    length, count = scale.shape[0], len(jobs)
    ins = [a if any(a is r for r in received.arrays) else in_vmem(a) for a in place.arrays]
    wide = jax.ShapeDtypeStruct((length, H * DV), BF16)
    narrow = jax.ShapeDtypeStruct((length, H * DK), BF16)
    return pl.pallas_call(
        functools.partial(cross_kernel, placed, near, scale_at),
        in_specs=[VMEM] * len(ins) + [HBM] * len(outs) + [VMEM] * len(after),
        out_specs=[HBM] * 4,
        out_shape=[wide, narrow, narrow, wide],
        input_output_aliases={len(ins) + i: i for i in range(len(outs))},
        scratch_shapes=[
            pltpu.VMEM((length, count * YW), BF16),
            pltpu.VMEM((length, count * XW), BF16),
            pltpu.SemaphoreType.DMA((count,)),
            pltpu.SemaphoreType.DMA((count,)),
        ],
        compiler_params=params(),
        name="near" if near else "far",
    )(*ins, *outs, *map(in_vmem, after))


def scan_sum(state, size, sign):
    def moved(array, step):
        return lax.ppermute(array, "ctx", [(i, i + sign * step) for i in range(size) if 0 <= i + sign * step < size])

    total, step = moved(state, 1), 1
    while step < size:
        total, step = total + moved(total, step), 2 * step
    return total


def local(queries, keys, values, out_grad):
    size = lax.axis_size("ctx")
    args = (queries, keys, values, out_grad)
    x1, y1, scale_low, scale_high, fa = load(*args)
    swap_x = functools.partial(lax.ppermute, axis_name="ctx", perm=[(0, 1), (1, 0), (2, 3), (3, 2)])
    swap_y = functools.partial(lax.ppermute, axis_name="ctx", perm=[(0, 2), (2, 0), (1, 3), (3, 1)])
    if size == 4:
        got_xa = swap_x(fa)
    x2, y2, f_steps, fb = f_states(*args, scale_high)
    if size == 4:
        got_y1 = swap_y(fb)
    x, y, g_steps, gs = g_states(*args, scale_low)
    g = pairs_of(x, y, g_steps)
    f = pairs_of(x1, y1, f_steps) + pairs_of(x2, y2, f_steps)
    parts, token = [], []
    if EARLY:
        parts.append(local_terms(f[:EARLY], g[:EARLY]))
        token = parts[0][:1]
    if size == 4:
        mixed = payload("mixed", lambda p, a, b: jnp.where(is_inner(), a[p], b[p]), HALF, (gs, fb), token)
        got_xb = swap_x(mixed)
        parts.append(local_terms(f[EARLY:LATE], g[EARLY:LATE], [mixed]))
        sum_a = payload("swapped", lambda p, a, b: a[p] + b[p], HALF, (fa, got_xa), parts[-1][:1])
        got_y2 = swap_y(sum_a)

        def summed(start, stop, after):
            def work(p, got, own):
                return got[start + p] + jnp.where(is_inner(), own[HALF + start + p], 0.0)

            return payload("summed", work, stop - start, (got_y1, gs), after)

        last = [summed(0, CUT, [sum_a])]
        got_last = [swap_x(last[0])]
        parts.append(local_terms(f[LATE:], g[LATE:], last))
        x1_steps = first_steps(x1, y1, last)
        last.append(summed(CUT, HALF, [parts[-1][0], x1_steps]))
        got_last.append(swap_x(last[1]))
        near = [(array, p, INNER) for array in (got_xa, got_xb) for p in range(HALF)]
        far = [((got_y2, p, ALWAYS), (got_xb, p, OUTER)) for p in range(HALF)]
        far += [((got_y1, p, ALWAYS), (got_last[p >= CUT], p % CUT, ALWAYS)) for p in range(HALF)]
        after = last[1:]
    else:
        parts += [local_terms(f[EARLY:LATE], g[EARLY:LATE]), local_terms(f[LATE:], g[LATE:])]
        x1_steps, after = first_steps(x1, y1, []), []
        near = [(array, p, ALWAYS) for array in [scan_sum(s, size, 1) for s in (fa, fb)] for p in range(HALF)]
        after_me = scan_sum(gs, size, -1)
        far = [((after_me, p, ALWAYS),) for p in range(PAIRS)]
    f[:HALF] = pairs_of(x1, y1, x1_steps)
    local_of = [(part, p) for part in parts for p in range(part[0].shape[1] // YW)]

    def jobs(pairs, side, other, results, terms):
        return [Job(side[p], other[p], local_of[p][0][results], local_of[p][0][results + 1], local_of[p][1], terms(p), p) for p in pairs]

    outs = cross_terms(jobs(range(PAIRS), g, f, 0, lambda p: (near[p],)), True, scale_low, [], after)
    for pairs in ORDER:
        outs = cross_terms(jobs(pairs, f, g, 2, lambda p: far[p]), False, scale_high, outs)
    return tuple(outs)


def solution(mesh):
    spec = P(("batch", "ctx"), None)
    return jax.shard_map(local, mesh=mesh, in_specs=(spec,) * 4, out_specs=(spec,) * 4, check_vma=False)
```
